512 devices in a mesh: dom: 16 (over x, y_lo, core), orb: 32 (over z, y_hi).
Axes of the slice: x: 4, y: 8 (y_hi: 4, y_lo: 2; y = y_hi * 2 + y_lo), z: 8, core: 2. Of those that a mesh axis runs over, the one named last changes fastest.
Arguments:
- orbitals: float32 [16, 64, 48, 2304], P('dom', 'orb'), may hold values from -6 to 6
- occupations: float32 [16, 64], P('dom', 'orb'), may hold values from 0.25 to 2
- occupied_count: int32 [16], P('dom'), may hold values from 16 to 64
- weights: float32 [16, 48], P('dom'), may hold values from 0 to 1, as said below
- external_potential: float32 [16, 48, 2304], P('dom'), may hold values from -2 to 0.5
- core_density: float32 [16, 48, 2304], P('dom'), may hold values from 0.08 to 2.88, as said below
- hartree_guess: float32 [512, 2304], P(('dom', 'orb')), may hold values from -6 to 6
Outputs:
- potential: float32 [512, 2304], P(('dom', 'orb'))
The draws below stay inside these ranges and needn't reach their ends.
Inputs may be any that keep to these rules, and one draw needn't show every extreme that they name: orbitals 0 to occupied_count - 1 of a domain are occupied. `weights`: positive; on every global plane the weights of the boxes that cover it sum to one. `core_density`: positive.
All inputs are finite; a program needn't handle non-finite values.
Results may differ from the reference program's by a relative error of at most 0.00017.
Values sent between devices are 32-bit elements; how exact they have to be, the bound alone decides.
No kernel may reach another device: no remote copies, remote signals or barrier semaphores. Data moves between devices by JAX's collectives and lax.ppermute only.
A program may use at most 64 MiB of HBM per device.

```python
import math
import jax
import jax.numpy as jnp
from jax import lax

SIDE = 48
CORE = 32
BUF = 8
DEGREE = 8
SWEEPS = 4
CYCLES = 2
DOMAINS = 16
ORBS = 64
BOX = 48
GX = 512


def draw_weights(key, part):
    samples = jnp.exp(jax.random.uniform(key, (DOMAINS, BOX), jnp.float32, -1.6094, 1.6094))
    position = (jnp.arange(DOMAINS, dtype=jnp.int32)[:, None] * CORE - BUF + jnp.arange(BOX, dtype=jnp.int32)[None, :]) % GX
    totals = jnp.zeros((GX,), jnp.float32).at[position.reshape(-1)].add(samples.reshape(-1))
    return samples / totals[position]


def draw_core_density(key, part):
    ladder = jnp.arange(DOMAINS, dtype=jnp.float32) / max(DOMAINS - 1, 1)
    scales = 0.3 * 3.0 ** ladder
    roughness = jax.random.uniform(key, (DOMAINS, BOX, SIDE * SIDE), jnp.float32, 0.4, 1.6)
    return scales[:, None, None] * roughness


def set_ends(drawn, key, smallest, high):
    dims = drawn.shape
    spot = [jax.random.randint(jax.random.fold_in(key, axis), (), 0, dims[axis]) for axis in range(len(dims))]
    drawn = drawn.at[tuple(spot)].set(smallest)
    longest = dims.index(max(dims))
    spot[longest] = (spot[longest] + 1) % dims[longest]
    return drawn.at[tuple(spot)].set(high)


def level_of(rng, shape, pieces, low, high):
    def one(axis_at, blocks):
        draws = jax.random.uniform(jax.random.fold_in(jax.random.fold_in(rng, 6), axis_at), (blocks,), jnp.float32, low / len(pieces), high / len(pieces))
        return jnp.repeat(jnp.exp(draws), shape[axis_at] // blocks).reshape((-1,) + (1,) * (len(shape) - axis_at - 1))

    factor_of = one(*pieces[0])
    for cut in pieces[1:]:
        factor_of = factor_of * one(*cut)
    return factor_of


def bell_draw(stream_key, extent, scale, most, shards=(), kind=jnp.bfloat16):
    gain = level_of(stream_key, extent, shards, -0.22, 0.18) if shards else 1.0
    array = jax.random.normal(stream_key, extent, jnp.float32) * scale * gain
    return jnp.minimum(jnp.maximum(array, -most), most).astype(kind)


def setup_inputs(seed: int = 0) -> dict:
    key_list = jax.random.split(jax.random.key(seed), 8)
    return {
        "orbitals": bell_draw(key_list[0], (DOMAINS, ORBS, BOX, SIDE * SIDE), 1.0, 6.0, ((0, 16), (1, 32)), jnp.float32),
        "occupations": jnp.clip(jnp.exp(math.log(2.0) - 2.0794415 * jax.random.uniform(key_list[1], (DOMAINS, ORBS), jnp.float32) ** level_of(key_list[1], (DOMAINS, ORBS), ((0, 16), (1, 32)), -0.2, 0.2)), 0.25, 2.0),
        "occupied_count": set_ends(jax.random.randint(key_list[2], (DOMAINS,), ORBS // 4, ORBS + 1), jax.random.fold_in(key_list[2], 1), ORBS // 4, ORBS).astype(jnp.int32),
        "weights": draw_weights(jax.random.fold_in(key_list[7], 71), 0),
        "external_potential": jnp.clip(-2.0 + 2.5 * jax.random.uniform(key_list[4], (DOMAINS, BOX, SIDE * SIDE), jnp.float32) ** level_of(key_list[4], (DOMAINS, BOX, SIDE * SIDE), ((0, 16),), -0.2, 0.2), -2.0, 0.5),
        "core_density": draw_core_density(jax.random.fold_in(key_list[7], 71), 0),
        "hartree_guess": bell_draw(key_list[6], (GX, SIDE * SIDE), 1.0, 6.0, ((0, 512),), jnp.float32),
    }


EXCHANGE_FACTOR = (3.0 / 3.141592653589793) ** (1.0 / 3.0)
FOUR_PI = 4.0 * 3.141592653589793
RELAXATION = 0.8
CUTOFF = 1.5

def transverse_sum(field):
    cells = field.shape[-1]
    column = jnp.arange(cells, dtype=jnp.int32) % SIDE
    left = jnp.where(column == 0, jnp.roll(field, -(SIDE - 1), -1), jnp.roll(field, 1, -1))
    right = jnp.where(column == SIDE - 1, jnp.roll(field, SIDE - 1, -1), jnp.roll(field, -1, -1))
    return left + right + jnp.roll(field, SIDE, -1) + jnp.roll(field, -SIDE, -1)

def hamiltonian(orbital_set, box_potential):
    padded = jnp.pad(orbital_set, ((0, 0), (1, 1), (0, 0)))
    neighbours = padded[:, 2:] + padded[:, :-2] + transverse_sum(orbital_set)
    return 0.5 * (6.0 * orbital_set - neighbours) + box_potential[None] * orbital_set

def chebyshev(orbital_set, box_potential):
    low_bound = jnp.min(box_potential) + CUTOFF
    high_bound = jnp.max(box_potential) + 6.0
    center = 0.5 * (high_bound + low_bound)
    half_width = 0.5 * (high_bound - low_bound)
    previous = orbital_set
    current = (hamiltonian(orbital_set, box_potential) - center * orbital_set) / half_width
    for step_index in range(DEGREE - 1):
        following = 2.0 * (hamiltonian(current, box_potential) - center * current) / half_width - previous
        previous, current = (current, following)
    return current

def reference(orbitals, occupations, occupied_count, weights, external_potential, core_density, hartree_guess):
    box_starts = jnp.arange(DOMAINS, dtype=jnp.int32) * CORE - BUF
    plane_index = (box_starts[:, None] + jnp.arange(BOX, dtype=jnp.int32)[None, :]) % GX
    occupied = jnp.arange(ORBS, dtype=jnp.int32)[None, :] < occupied_count[:, None]
    factors = jnp.where(occupied, occupations, jnp.float32(0.0)) / ORBS
    orbital_set = orbitals
    hartree = hartree_guess
    scf_box = jnp.zeros_like(external_potential)
    potential = hartree_guess
    for cycle_index in range(CYCLES):
        box_potential = external_potential + scf_box

        def one_domain(domain_item):
            domain_orbitals, domain_potential, factor_row = domain_item
            filtered = chebyshev(domain_orbitals, domain_potential)
            squares = lax.optimization_barrier(jnp.mean(filtered * filtered, axis=(1, 2))) + 1e-06
            filtered = filtered / jnp.sqrt(squares)[:, None, None]
            density_part = lax.optimization_barrier(jnp.sum(factor_row[:, None, None] * filtered * filtered, axis=0))
            return (filtered, density_part)
        orbital_set, density_part = lax.map(one_domain, (orbital_set, box_potential, factors))
        weighted = (density_part + core_density) * weights[:, :, None]
        density = jnp.zeros((GX, SIDE * SIDE), jnp.float32).at[plane_index.reshape(-1)].add(weighted.reshape(-1, SIDE * SIDE))
        average = jnp.mean(density)
        source = FOUR_PI * (density - average)
        for sweep_index in range(SWEEPS):
            neighbours = jnp.roll(hartree, 1, 0) + jnp.roll(hartree, -1, 0) + transverse_sum(hartree)
            hartree = hartree + RELAXATION * ((neighbours + source) / 6.0 - hartree)
        potential = hartree - EXCHANGE_FACTOR * jnp.cbrt(density)
        scf_box = potential[plane_index]
    return potential
```

```python
import functools

import jax
import jax.numpy as jnp
from jax import lax
from jax.experimental import pallas as pl
from jax.experimental.pallas import tpu as pltpu
from jax.sharding import PartitionSpec as P

SIDE = 48
CORE = 32
BUF = 8
DEGREE = 8
SWEEPS = 4
BOX = 48
CELLS = SIDE * SIDE
LANES = 128
COLS = CELLS // LANES
PAD = 8
EXT = 64

EXCHANGE_FACTOR = (3.0 / 3.141592653589793) ** (1.0 / 3.0)
FOUR_PI = 4.0 * 3.141592653589793
RELAXATION = 0.8
CUTOFF = 1.5
KEEP = 1.0 - RELAXATION
SPREAD = RELAXATION / 6.0
SOURCE = SPREAD * FOUR_PI


def masks():
    lane = lax.broadcasted_iota(jnp.int32, (8, LANES), 1)
    row = lax.broadcasted_iota(jnp.int32, (8, LANES), 0)
    first = [(lane + LANES * i) % SIDE == 0 for i in range(3)]
    last = [(lane + LANES * i) % SIDE == SIDE - 1 for i in range(3)]
    return dict(lane=lane, row=row, first=first, last=last)


def shifted(pieces, shift, m):
    whole, part = divmod(shift, LANES)
    turned = [pltpu.roll(p, part, 1) for p in pieces]
    keep = m["lane"] >= part
    n = len(pieces)
    return [jnp.where(keep, turned[(i - whole) % n], turned[(i - whole - 1) % n]) for i in range(n)]


def neighbour_sum(above, here, below, m):
    left = shifted(here, 1, m)
    right = shifted(here, -1, m)
    left_wrap = [jnp.where(m["first"][i % 3], left[i], 0.0) for i in range(COLS)]
    left_rest = [jnp.where(m["first"][i % 3], 0.0, left[i]) for i in range(COLS)]
    right_wrap = [jnp.where(m["last"][i % 3], right[i], 0.0) for i in range(COLS)]
    right_rest = [jnp.where(m["last"][i % 3], 0.0, right[i]) for i in range(COLS)]
    down = shifted([here[i] + left_wrap[i] for i in range(COLS)], -SIDE, m)
    up = shifted([here[i] + right_wrap[i] for i in range(COLS)], SIDE, m)
    out = []
    for i in range(COLS):
        before = pltpu.roll(jnp.where(m["row"] == 7, above[i], here[i]), 1, 0)
        after = pltpu.roll(jnp.where(m["row"] == 0, below[i], here[i]), 7, 0)
        out.append(((left_rest[i] + right_rest[i]) + (down[i] + up[i])) + (before + after))
    return out


def pieces_of(ref, lead, start):
    rows = pl.ds(start if isinstance(start, int) else pl.multiple_of(start, 8), 8)
    return [ref[(*lead, rows, pl.ds(LANES * i, LANES))] for i in range(COLS)]


def put_pieces(ref, lead, start, pieces):
    rows = pl.ds(start if isinstance(start, int) else pl.multiple_of(start, 8), 8)
    for i in range(COLS):
        ref[(*lead, rows, pl.ds(LANES * i, LANES))] = pieces[i]


def sum_at(ref, lead, start, m):
    above, here, below = (pieces_of(ref, lead, start + k) for k in (-8, 0, 8))
    return here, neighbour_sum(above, here, below, m)


def run_filter(psi_ref, a_ref, b_ref, w_ref, v_tile, m):
    orbs = psi_ref.shape[0]
    low = high = None
    for t in range(BOX // 8):
        for v in v_tile(8 * t):
            low = v if low is None else jnp.minimum(low, v)
            high = v if high is None else jnp.maximum(high, v)
    low = jnp.min(low, keepdims=True) + CUTOFF
    high = jnp.max(high, keepdims=True) + 6.0
    center = 0.5 * (high + low)
    inverse = 1.0 / (0.5 * (high - low))
    offset = (3.0 - center) * (2.0 * inverse)
    double = jnp.broadcast_to(2.0 * inverse, (8, LANES))
    single = jnp.broadcast_to(inverse, (8, LANES))
    offset = jnp.broadcast_to(offset, (8, LANES))
    for t in range(BOX // 8):
        put_pieces(w_ref, (), 8 * t, [double * v + offset for v in v_tile(8 * t)])
    zero = jnp.zeros((PAD, CELLS), jnp.float32)
    for q in range(orbs):
        for ref in (a_ref, b_ref):
            ref[q, 0:PAD, :] = zero
            ref[q, PAD + BOX : PAD + BOX + PAD, :] = zero
        a_ref[q, PAD : PAD + BOX, :] = psi_ref[q]

    def step(source, target, first):
        def tile(t, carry):
            w = pieces_of(w_ref, (), 8 * t)
            for q in range(orbs):
                here, around = sum_at(source, (q,), PAD + 8 * t, m)
                new = [w[i] * here[i] - single * around[i] for i in range(COLS)]
                if first:
                    new = [0.5 * n for n in new]
                else:
                    old = pieces_of(target, (q,), PAD + 8 * t)
                    new = [new[i] - old[i] for i in range(COLS)]
                put_pieces(target, (q,), PAD + 8 * t, new)
            return carry

        lax.fori_loop(0, BOX // 8, tile, 0)

    step(a_ref, b_ref, True)

    def pair(k, carry):
        step(b_ref, a_ref, False)
        step(a_ref, b_ref, False)
        return carry

    lax.fori_loop(0, (DEGREE - 2) // 2, pair, 0)
    step(b_ref, a_ref, False)


def norms(a_ref, orbs):
    out = []
    for q in range(orbs):
        total = [jnp.zeros((8, LANES), jnp.float32) for _ in range(3)]
        for t in range(BOX // 8):
            for i, y in enumerate(pieces_of(a_ref, (q,), PAD + 8 * t)):
                total[i % 3] = total[i % 3] + y * y
        mean = jnp.sum(total[0] + total[1] + total[2], keepdims=True) * (1.0 / (BOX * CELLS))
        out.append(jnp.broadcast_to(lax.rsqrt(mean + 1e-06), (8, LANES)))
    return out


def density_tile(a_ref, scale, factor_ref, core_ref, weight_ref, t, share, psi_out):
    weight = jnp.broadcast_to(weight_ref[8 * t : 8 * t + 8, :], (8, LANES))
    total = [share * c for c in pieces_of(core_ref, (0,), 8 * t)]
    for q in range(len(scale)):
        y = [p * scale[q] for p in pieces_of(a_ref, (q,), PAD + 8 * t)]
        if psi_out is not None:
            put_pieces(psi_out, (q,), 8 * t, y)
        total = [total[i] + factor_ref[q] * (y[i] * y[i]) for i in range(COLS)]
    return [weight * d for d in total]


def first_kernel(share, factor_ref, psi_ref, ext_ref, core_ref, weight_ref, psi_out, own_out, up_out, a_ref, b_ref, w_ref):
    m = masks()
    run_filter(psi_ref.at[0], a_ref, b_ref, w_ref, lambda r: pieces_of(ext_ref, (0,), r), m)
    scale = norms(a_ref, psi_ref.shape[1])
    for t in range(BOX // 8):
        tile = density_tile(a_ref, scale, factor_ref, core_ref, weight_ref, t, share, psi_out)
        if t < 3:
            put_pieces(own_out, (), 8 * t, tile)
        else:
            put_pieces(up_out, (), 8 * (t - 3), tile)


def sweep(source, target, density, m):
    def tile(t, carry):
        here, around = sum_at(source, (), PAD + 8 * t, m)
        new = [KEEP * here[i] + SPREAD * around[i] for i in range(COLS)]
        if density is not None:
            push = pieces_of(density, (), 8 * t)
            new = [new[i] + SOURCE * push[i] for i in range(COLS)]
        put_pieces(target, (), PAD + 8 * t, new)
        return carry

    lax.fori_loop(0, EXT // 8, tile, 0)


def second_kernel(
    share, factor_ref, psi_ref, ext_ref, core_ref, weight_ref, before_ref, guess_ref, after_ref, low_ref, high_ref,
    hartree_out, core_out, smooth_out, up_out, down_out, charge_out,
    a_ref, b_ref, w_ref, g_ref, h_ref, d_ref,
):
    m = masks()
    orbs = psi_ref.shape[0]
    zero = jnp.zeros((PAD, CELLS), jnp.float32)
    for ref in (g_ref, h_ref):
        ref[0:PAD, :] = zero
        ref[PAD + EXT : PAD + EXT + PAD, :] = zero
    g_ref[PAD : PAD + 16, :] = before_ref[...]
    g_ref[PAD + 16 : PAD + 48, :] = guess_ref[...]
    g_ref[PAD + 48 : PAD + 64, :] = after_ref[...]
    d_ref[0:32, :] = low_ref[...]
    d_ref[32:64, :] = high_ref[...]
    for _ in range(SWEEPS // 2):
        sweep(g_ref, h_ref, d_ref, m)
        sweep(h_ref, g_ref, d_ref, m)
    hartree_out[...] = g_ref[PAD : PAD + EXT, :]
    charge = [jnp.zeros((8, LANES), jnp.float32) for _ in range(3)]
    for t in range(4):
        for i, d in enumerate(pieces_of(d_ref, (), 8 * t)):
            charge[i % 3] = charge[i % 3] + d
    frame_charge = (charge[0] + charge[1] + charge[2]) * share
    for t in range(BOX // 8):
        density = pieces_of(d_ref, (), 8 + 8 * t)
        hartree = pieces_of(g_ref, (), PAD + 8 + 8 * t)
        ionic = pieces_of(ext_ref, (0,), 8 * t)
        new = [
            ionic[i] + (hartree[i] - EXCHANGE_FACTOR * jnp.exp(jnp.log(density[i]) * (1.0 / 3.0)))
            for i in range(COLS)
        ]
        put_pieces(h_ref, (), PAD + 8 * t, new)
    run_filter(psi_ref, a_ref, b_ref, w_ref, lambda r: pieces_of(h_ref, (), PAD + r), m)
    scale = norms(a_ref, orbs)
    for ref in (g_ref, h_ref):
        ref[PAD : PAD + 8, :] = zero
        ref[PAD + 56 : PAD + 64, :] = zero
    d_ref[0:8, :] = zero
    d_ref[56:64, :] = zero
    charge = [frame_charge] + [jnp.zeros((8, LANES), jnp.float32) for _ in range(2)]
    for t in range(BOX // 8):
        tile = density_tile(a_ref, scale, factor_ref, core_ref, weight_ref, t, share, None)
        put_pieces(d_ref, (), 8 + 8 * t, tile)
        put_pieces(g_ref, (), PAD + 8 + 8 * t, [SOURCE * d for d in tile])
        if t == 0:
            put_pieces(down_out, (), 0, tile)
        elif t == 5:
            put_pieces(up_out, (), 0, tile)
        else:
            put_pieces(core_out, (), 8 * (t - 1), tile)
        for i, d in enumerate(tile):
            charge[i % 3] = charge[i % 3] + d
    charge_out[...] = jnp.broadcast_to(jnp.sum(charge[0] + charge[1] + charge[2], keepdims=True), charge_out.shape)
    sweep(g_ref, h_ref, d_ref, m)
    sweep(h_ref, g_ref, d_ref, m)
    sweep(g_ref, h_ref, d_ref, m)
    down_out[8:24, :] = h_ref[PAD : PAD + 16, :]
    smooth_out[...] = h_ref[PAD + 16 : PAD + 48, :]
    up_out[8:24, :] = h_ref[PAD + 48 : PAD + 64, :]


def decay_kernel(hartree_ref, out_ref, g_ref, h_ref):
    m = masks()
    zero = jnp.zeros((PAD, CELLS), jnp.float32)
    for ref in (g_ref, h_ref):
        ref[0:PAD, :] = zero
        ref[PAD + EXT : PAD + EXT + PAD, :] = zero
    g_ref[PAD : PAD + EXT, :] = hartree_ref[...]
    for _ in range(SWEEPS // 2):
        sweep(g_ref, h_ref, None, m)
        sweep(h_ref, g_ref, None, m)
    out_ref[...] = g_ref[PAD + 16 : PAD + 48, :]


VMEM = pl.BlockSpec(memory_space=pltpu.VMEM)
SMEM = pl.BlockSpec(memory_space=pltpu.SMEM)
LIMIT = pltpu.CompilerParams(vmem_limit_bytes=40 * 2**20)


def f32(*shape):
    return jax.ShapeDtypeStruct(shape, jnp.float32)


def body(orbitals, occupations, occupied_count, weights, external_potential, core_density, hartree_guess):
    orb_count = lax.axis_size("orb")
    dom_count = lax.axis_size("dom")
    orb_rank = lax.axis_index("orb")
    per_device = orbitals.shape[1]
    rank = orb_rank * per_device + jnp.arange(per_device, dtype=jnp.int32)
    factors = jnp.where(rank < occupied_count[0], occupations[0], jnp.float32(0.0)) / (per_device * orb_count)
    weight = weights.reshape(BOX, 1)
    share = 1.0 / orb_count
    up = [(i, (i + 1) % dom_count) for i in range(dom_count)]
    down = [(j, i) for i, j in up]
    filter_scratch = [
        pltpu.VMEM((per_device, BOX + 2 * PAD, CELLS), jnp.float32),
        pltpu.VMEM((per_device, BOX + 2 * PAD, CELLS), jnp.float32),
        pltpu.VMEM((BOX, CELLS), jnp.float32),
    ]
    field = pltpu.VMEM((EXT + 2 * PAD, CELLS), jnp.float32)

    psi, own, upper = pl.pallas_call(
        functools.partial(first_kernel, share),
        in_specs=[SMEM] + [VMEM] * 4,
        out_specs=[VMEM] * 3,
        out_shape=[f32(per_device, BOX, CELLS), f32(24, CELLS), f32(24, CELLS)],
        scratch_shapes=filter_scratch,
        compiler_params=LIMIT,
        name="first",
    )(factors, orbitals, external_potential, core_density, weight)

    behind = lax.ppermute(upper, "dom", up)
    frame = jnp.concatenate([behind[:8], own[:16] + behind[8:], own[16:]], axis=0)
    sent = jnp.concatenate(
        [frame[:, None], jnp.broadcast_to(hartree_guess[None], (orb_count, 1, CELLS))], axis=2
    )
    arrived = lax.all_to_all(sent, "orb", 0, 0, tiled=True)
    plane = arrived[:, :, :CELLS].sum(axis=0)
    guess = arrived[:, 0, CELLS:]
    guess_before = lax.ppermute(guess[16:], "dom", up)
    guess_after = lax.ppermute(guess[:16], "dom", down)
    low = lax.all_to_all(jnp.broadcast_to(plane[None], (orb_count, 1, CELLS)), "orb", 0, 0, tiled=True)
    low = low.reshape(CORE, CELLS)
    high = lax.ppermute(low, "dom", down)

    hartree, core, smooth, upper, lower, charge = pl.pallas_call(
        functools.partial(second_kernel, share),
        in_specs=[SMEM] + [VMEM] * 9,
        out_specs=[VMEM] * 6,
        out_shape=[
            f32(EXT, CELLS), f32(CORE, CELLS), f32(CORE, CELLS), f32(24, CELLS), f32(24, CELLS), f32(1, LANES)
        ],
        scratch_shapes=filter_scratch + [field, field, pltpu.VMEM((EXT, CELLS), jnp.float32)],
        compiler_params=LIMIT,
        name="second",
    )(factors, psi, external_potential, core_density, weight, guess_before, guess, guess_after, low, high)

    charge = lax.all_to_all(jnp.broadcast_to(charge[None], (dom_count, 1, LANES)), "dom", 0, 0, tiled=True)
    from_below = lax.ppermute(upper, "dom", up)
    from_above = lax.ppermute(lower, "dom", down)
    charge = charge.sum(axis=0)
    core = jnp.concatenate([core[:8] + from_below[:8], core[8:24], core[24:] + from_above[:8]], axis=0)
    smooth = smooth + jnp.concatenate([from_below[8:], from_above[8:]], axis=0)
    sent = jnp.concatenate(
        [core[:, None], smooth[:, None], jnp.broadcast_to(charge[None], (orb_count, 1, LANES))], axis=2
    )
    arrived = lax.all_to_all(sent, "orb", 0, 0, tiled=True)

    settled = pl.pallas_call(
        decay_kernel,
        in_specs=[VMEM],
        out_specs=VMEM,
        out_shape=f32(CORE, CELLS),
        scratch_shapes=[field, field],
        compiler_params=LIMIT,
        name="decay",
    )(hartree)
    settled = lax.dynamic_slice_in_dim(settled, orb_rank, 1, 0)

    total = arrived.sum(axis=0)
    density = total[:, :CELLS]
    average = total[:, 2 * CELLS : 2 * CELLS + 1] / (dom_count * CORE * CELLS)
    return settled + total[:, CELLS : 2 * CELLS] - (SWEEPS * SOURCE) * average - EXCHANGE_FACTOR * jnp.cbrt(density)


def solution(mesh):
    placed = (
        P("dom", "orb", None, None),
        P("dom", "orb"),
        P("dom"),
        P("dom", None),
        P("dom", None, None),
        P("dom", None, None),
        P(("dom", "orb"), None),
    )
    return jax.shard_map(
        body, mesh=mesh, in_specs=placed, out_specs=P(("dom", "orb"), None), check_vma=False
    )
```

```python
import functools

import jax
import jax.numpy as jnp
from jax import lax
from jax.experimental import pallas as pl
from jax.experimental.pallas import tpu as pltpu
from jax.sharding import PartitionSpec as P

SIDE = 48
CORE = 32
BUF = 8
DEGREE = 8
SWEEPS = 4
BOX = 48
CELLS = SIDE * SIDE
LANES = 128
COLS = CELLS // LANES
PAD = 8
EXT = 64
SHIFT = 12
UP = 20
BLOCK = 384
BLOCKS = CELLS // BLOCK
DEPTH = BLOCK + LANES
TILE = 16

EXCHANGE_FACTOR = (3.0 / 3.141592653589793) ** (1.0 / 3.0)
FOUR_PI = 4.0 * 3.141592653589793
RELAXATION = 0.8
CUTOFF = 1.5
KEEP = 1.0 - RELAXATION
SPREAD = RELAXATION / 6.0
SOURCE = SPREAD * FOUR_PI


def build_neighbours(matrix_ref):
    rows = lax.broadcasted_iota(jnp.int32, (DEPTH, BLOCK), 0)
    cols = lax.broadcasted_iota(jnp.int32, (DEPTH, BLOCK), 1)
    edge = rows - BLOCK
    inside = rows < BLOCK
    after = edge < SIDE
    before = edge >= LANES - SIDE
    row_y = jnp.where(inside, rows // SIDE, jnp.where(after, SIDE // 6, jnp.where(before, -1, -9)))
    row_x = jnp.where(inside, rows % SIDE, jnp.where(after, edge, edge - (LANES - SIDE)))
    col_y = cols // SIDE
    col_x = cols % SIDE
    gap_x = jnp.abs(row_x - col_x)
    along = (row_y == col_y) & ((gap_x == 1) | (gap_x == SIDE - 1))
    across = (row_x == col_x) & (jnp.abs(row_y - col_y) == 1)
    ones = jnp.where(along | across, 1.0, 0.0).astype(jnp.bfloat16)
    matrix_ref[0:DEPTH, :] = ones
    matrix_ref[DEPTH : 2 * DEPTH, :] = ones


def tile_of(ref, start):
    return [ref[pl.ds(start, 8), pl.ds(LANES * i, LANES)] for i in range(COLS)]


def put_tile(ref, start, pieces):
    for i in range(COLS):
        ref[pl.ds(start, 8), pl.ds(LANES * i, LANES)] = pieces[i]


def put_split(split_ref, planes, start, upper, lower):
    lane = lax.broadcasted_iota(jnp.int32, (TILE, LANES), 1)
    both = [jnp.concatenate([upper[i], lower[i]], axis=0) for i in range(COLS)]
    high = [x.astype(jnp.bfloat16) for x in both]
    low = [(both[i] - high[i].astype(jnp.float32)).astype(jnp.bfloat16) for i in range(COLS)]
    for b in range(BLOCKS):
        rows = pl.ds(b * planes + start, TILE)
        for k, half in enumerate((high, low)):
            base = k * DEPTH
            for j in range(3):
                split_ref[rows, pl.ds(base + LANES * j, LANES)] = half[3 * b + j]
            edge = jnp.where(lane < SIDE, half[(3 * b + 3) % COLS], half[(3 * b - 1) % COLS])
            split_ref[rows, pl.ds(base + BLOCK, LANES)] = edge


def multiply(split_ref, matrix_ref, sum_ref, rows):
    sum_ref[0:rows, :] = jnp.dot(
        split_ref[0:rows, :], matrix_ref[...], preferred_element_type=jnp.float32
    )


def sum_tile(sum_ref, planes, start):
    return [
        sum_ref[pl.ds((i // 3) * planes + start, 8), pl.ds(LANES * (i % 3), LANES)] for i in range(COLS)
    ]


def around(flat, before, here, after):
    row = lax.broadcasted_iota(jnp.int32, (8, LANES), 0)
    out = []
    for i in range(COLS):
        lower = pltpu.roll(jnp.where(row == 7, before[i], here[i]), 1, 0)
        upper = pltpu.roll(jnp.where(row == 0, after[i], here[i]), 7, 0)
        out.append(flat[i] + (lower + upper))
    return out


def clear_pads(refs, planes):
    zero = jnp.zeros((PAD, CELLS), jnp.float32)
    for ref in refs:
        ref[0:PAD, :] = zero
        ref[PAD + planes : 2 * PAD + planes, :] = zero


def split_all(source, split_ref, planes):
    for s in range(0, planes, TILE):
        put_split(split_ref, planes, s, tile_of(source, PAD + s), tile_of(source, PAD + s + 8))


def update(source, target, split_ref, sum_ref, planes, rule):
    for s in range(0, planes, TILE):
        tiles = [tile_of(source, PAD + s + 8 * k) for k in range(-1, 3)]
        new = []
        for k in range(2):
            total = around(sum_tile(sum_ref, planes, s + 8 * k), *tiles[k : k + 3])
            new.append(rule(s + 8 * k, tiles[k + 1], total))
            put_tile(target, PAD + s + 8 * k, new[k])
        if split_ref is not None:
            put_split(split_ref, planes, s, *new)


def scaled_potential(v_tile, w_ref):
    low = high = None
    for t in range(BOX // 8):
        for v in v_tile(8 * t):
            low = v if low is None else jnp.minimum(low, v)
            high = v if high is None else jnp.maximum(high, v)
    low = jnp.min(low, keepdims=True) + CUTOFF
    high = jnp.max(high, keepdims=True) + 6.0
    center = 0.5 * (high + low)
    inverse = 1.0 / (0.5 * (high - low))
    offset = jnp.broadcast_to((3.0 - center) * (2.0 * inverse), (8, LANES))
    double = jnp.broadcast_to(2.0 * inverse, (8, LANES))
    for t in range(BOX // 8):
        put_tile(w_ref, 8 * t, [double * v + offset for v in v_tile(8 * t)])
    return jnp.broadcast_to(inverse, (8, LANES))


def run_filter(a_refs, b_refs, splits, sums, matrix_ref, w_ref, single):
    orbs = len(a_refs)

    def first_rule(q):
        def rule(r, here, total):
            w = tile_of(w_ref, r)
            return [0.5 * (w[i] * here[i] - single * total[i]) for i in range(COLS)]

        return rule

    def next_rule(q, target):
        def rule(r, here, total):
            w = tile_of(w_ref, r)
            old = tile_of(target[q], PAD + r)
            return [(w[i] * here[i] - single * total[i]) - old[i] for i in range(COLS)]

        return rule

    def step(source, target, rules, last=False):
        for q in range(orbs):
            multiply(splits[q], matrix_ref, sums[q], BLOCKS * BOX)
        for q in range(orbs):
            update(source[q], target[q], None if last else splits[q], sums[q], BOX, rules(q))

    for q in range(orbs):
        split_all(a_refs[q], splits[q], BOX)
    step(a_refs, b_refs, first_rule)

    def pair(k, carry):
        step(b_refs, a_refs, lambda q: next_rule(q, a_refs))
        step(a_refs, b_refs, lambda q: next_rule(q, b_refs))
        return carry

    lax.fori_loop(0, (DEGREE - 2) // 2, pair, 0)
    step(b_refs, a_refs, lambda q: next_rule(q, a_refs), last=True)


def norms(a_refs):
    out = []
    for ref in a_refs:
        total = [jnp.zeros((8, LANES), jnp.float32) for _ in range(3)]
        for t in range(BOX // 8):
            for i, y in enumerate(tile_of(ref, PAD + 8 * t)):
                total[i % 3] = total[i % 3] + y * y
        mean = jnp.sum(total[0] + total[1] + total[2], keepdims=True) * (1.0 / (BOX * CELLS))
        out.append(jnp.broadcast_to(lax.rsqrt(mean + 1e-06), (8, LANES)))
    return out


def density_tile(a_refs, scale, factor_ref, core_ref, weight_ref, t, share, psi_out):
    weight = jnp.broadcast_to(weight_ref[8 * t : 8 * t + 8, :], (8, LANES))
    total = [share * c for c in tile_of(core_ref, 8 * t)]
    for q, ref in enumerate(a_refs):
        y = [p * scale[q] for p in tile_of(ref, PAD + 8 * t)]
        if psi_out is not None:
            put_tile(psi_out.at[q], 8 * t, y)
        total = [total[i] + factor_ref[q] * (y[i] * y[i]) for i in range(COLS)]
    return [weight * d for d in total]


def relax(plane_ref, row, g_ref, h_ref, d_ref, split_ref, sum_ref, matrix_ref):
    clear_pads((g_ref, h_ref), EXT)
    g_ref[PAD : PAD + EXT, :] = jnp.zeros((EXT, CELLS), jnp.float32)
    g_ref[pl.ds(PAD + row, 1), :] = plane_ref[...]

    def rule(r, here, total):
        push = tile_of(d_ref, r)
        return [KEEP * here[i] + SPREAD * total[i] + SOURCE * push[i] for i in range(COLS)]

    def one(source, target, last=False):
        multiply(split_ref, matrix_ref, sum_ref, BLOCKS * EXT)
        update(source, target, None if last else split_ref, sum_ref, EXT, rule)

    split_all(g_ref, split_ref, EXT)
    for k in range(SWEEPS // 2):
        one(g_ref, h_ref)
        one(h_ref, g_ref, last=k == SWEEPS // 2 - 1)


def first_kernel(
    share, factor_ref, rank_ref, orbitals_ref, ext_ref, core_ref, weight_ref, guess_ref,
    psi_out, frame_out, smooth_out, up_out,
    a0, a1, b0, b1, x0, x1, s0, s1, w_ref, g_ref, h_ref, d_ref, matrix_ref, v_ref, c_ref, sem,
):
    copies = [
        pltpu.make_async_copy(ext_ref.at[0], v_ref, sem.at[0]),
        pltpu.make_async_copy(orbitals_ref.at[0, 0], a0.at[PAD : PAD + BOX], sem.at[1]),
        pltpu.make_async_copy(orbitals_ref.at[0, 1], a1.at[PAD : PAD + BOX], sem.at[2]),
        pltpu.make_async_copy(core_ref.at[0], c_ref, sem.at[3]),
    ]
    for copy in copies:
        copy.start()
    build_neighbours(matrix_ref)
    clear_pads((a0, a1, b0, b1), BOX)
    copies[0].wait()
    single = scaled_potential(lambda r: tile_of(v_ref, r), w_ref)
    copies[1].wait()
    copies[2].wait()
    run_filter((a0, a1), (b0, b1), (x0, x1), (s0, s1), matrix_ref, w_ref, single)
    scale = norms((a0, a1))
    copies[3].wait()
    zero = jnp.zeros((8, CELLS), jnp.float32)
    d_ref[0:8, :] = zero
    d_ref[56:64, :] = zero
    for t in range(BOX // 8):
        put_tile(d_ref, 8 + 8 * t, density_tile((a0, a1), scale, factor_ref, c_ref, weight_ref, t, share, psi_out))
    relax(guess_ref, 16 + rank_ref[0], g_ref, h_ref, d_ref, x0, s0, matrix_ref)
    low = 16 - SHIFT
    frame_out[...] = d_ref[low : low + CORE, :]
    smooth_out[...] = g_ref[PAD + low : PAD + low + CORE, :]
    up_out[0:UP, :] = d_ref[low + CORE : low + CORE + UP, :]
    up_out[UP : 48, :] = g_ref[PAD + low + CORE : PAD + EXT, :]


def second_kernel(
    share, factor_ref, rank_ref, psi_ref, ext_ref, core_ref, weight_ref, plane_ref, low_ref, high_ref,
    core_out, smooth_out, up_out, down_out, charge_out,
    a0, a1, b0, b1, x0, x1, s0, s1, w_ref, g_ref, h_ref, d_ref, matrix_ref,
):
    build_neighbours(matrix_ref)
    clear_pads((a0, a1, b0, b1), BOX)
    a0[PAD : PAD + BOX, :] = psi_ref[0]
    a1[PAD : PAD + BOX, :] = psi_ref[1]
    first = SHIFT - BUF
    h_ref[0 : CORE - first, :] = low_ref[first:CORE, :]
    h_ref[CORE - first : BOX, :] = high_ref[...]
    for t in range(BOX // 8):
        ionic = tile_of(ext_ref, 8 * t)
        own = tile_of(h_ref, 8 * t)
        put_tile(h_ref, 8 * t, [ionic[i] + own[i] for i in range(COLS)])
    single = scaled_potential(lambda r: tile_of(h_ref, r), w_ref)
    run_filter((a0, a1), (b0, b1), (x0, x1), (s0, s1), matrix_ref, w_ref, single)
    scale = norms((a0, a1))
    zero = jnp.zeros((8, CELLS), jnp.float32)
    d_ref[0:8, :] = zero
    d_ref[56:64, :] = zero
    charge = [jnp.zeros((8, LANES), jnp.float32) for _ in range(3)]
    for t in range(BOX // 8):
        tile = density_tile((a0, a1), scale, factor_ref, core_ref, weight_ref, t, share, None)
        put_tile(d_ref, 8 + 8 * t, tile)
        for i, d in enumerate(tile):
            charge[i % 3] = charge[i % 3] + d
    charge_out[...] = jnp.broadcast_to(jnp.sum(charge[0] + charge[1] + charge[2], keepdims=True), charge_out.shape)
    relax(plane_ref, 16 - SHIFT + rank_ref[0], g_ref, h_ref, d_ref, x0, s0, matrix_ref)
    core_out[...] = d_ref[16:48, :]
    down_out[0:8, :] = d_ref[8:16, :]
    up_out[0:8, :] = d_ref[48:56, :]
    down_out[8:24, :] = g_ref[PAD : PAD + 16, :]
    smooth_out[...] = g_ref[PAD + 16 : PAD + 48, :]
    up_out[8:24, :] = g_ref[PAD + 48 : PAD + 64, :]


VMEM = pl.BlockSpec(memory_space=pltpu.VMEM)
SMEM = pl.BlockSpec(memory_space=pltpu.SMEM)
ANY = pl.BlockSpec(memory_space=pl.ANY)
LIMIT = pltpu.CompilerParams(vmem_limit_bytes=48 * 2**20)


def f32(*shape):
    return jax.ShapeDtypeStruct(shape, jnp.float32)


def body(orbitals, occupations, occupied_count, weights, external_potential, core_density, hartree_guess):
    orb_count = lax.axis_size("orb")
    dom_count = lax.axis_size("dom")
    orb_rank = lax.axis_index("orb")
    per_device = orbitals.shape[1]
    rank = orb_rank * per_device + jnp.arange(per_device, dtype=jnp.int32)
    factors = jnp.where(rank < occupied_count[0], occupations[0], jnp.float32(0.0)) / (per_device * orb_count)
    weight = weights.reshape(BOX, 1)
    place = orb_rank.reshape(1)
    share = 1.0 / orb_count
    up = [(i, (i + 1) % dom_count) for i in range(dom_count)]
    down = [(j, i) for i, j in up]
    padded = pltpu.VMEM((BOX + 2 * PAD, CELLS), jnp.float32)
    wide = pltpu.VMEM((EXT + 2 * PAD, CELLS), jnp.float32)
    split = pltpu.VMEM((BLOCKS * EXT, 2 * DEPTH), jnp.bfloat16)
    sums = pltpu.VMEM((BLOCKS * EXT, BLOCK), jnp.float32)
    box = pltpu.VMEM((BOX, CELLS), jnp.float32)
    scratch = [padded] * 4 + [split] * 2 + [sums] * 2 + [
        box, wide, wide, pltpu.VMEM((EXT, CELLS), jnp.float32), pltpu.VMEM((2 * DEPTH, BLOCK), jnp.bfloat16)
    ]

    psi, frame, smooth, upper = pl.pallas_call(
        functools.partial(first_kernel, share),
        in_specs=[SMEM] * 2 + [ANY] * 3 + [VMEM] * 2,
        out_specs=[VMEM] * 4,
        out_shape=[f32(per_device, BOX, CELLS), f32(CORE, CELLS), f32(CORE, CELLS), f32(48, CELLS)],
        scratch_shapes=scratch + [box, box, pltpu.SemaphoreType.DMA((4,))],
        compiler_params=LIMIT,
        name="first",
    )(factors, place, orbitals, external_potential, core_density, weight, hartree_guess)

    behind = lax.ppermute(upper, "dom", up)
    frame = jnp.concatenate([frame[:UP] + behind[:UP], frame[UP:]], axis=0)
    smooth = jnp.concatenate([smooth[:28] + behind[UP:], smooth[28:]], axis=0)
    sent = jnp.concatenate([frame[:, None], smooth[:, None]], axis=2)
    arrived = lax.all_to_all(sent, "orb", 0, 0, tiled=True)
    total = arrived.sum(axis=0)
    owned_density = total[:, :CELLS]
    owned_hartree = total[:, CELLS:]
    plane = owned_hartree - EXCHANGE_FACTOR * jnp.cbrt(owned_density)
    low = lax.all_to_all(jnp.broadcast_to(plane[None], (orb_count, 1, CELLS)), "orb", 0, 0, tiled=True)
    low = low.reshape(CORE, CELLS)
    high = lax.ppermute(low[:UP], "dom", down)

    core, smooth, upper, lower, charge = pl.pallas_call(
        functools.partial(second_kernel, share),
        in_specs=[SMEM] * 2 + [VMEM] * 7,
        out_specs=[VMEM] * 5,
        out_shape=[f32(CORE, CELLS), f32(CORE, CELLS), f32(24, CELLS), f32(24, CELLS), f32(1, LANES)],
        scratch_shapes=scratch,
        compiler_params=LIMIT,
        name="second",
    )(factors, place, psi, external_potential[0], core_density[0], weight, owned_hartree, low, high)

    charge = charge + jnp.sum(owned_density)
    charge = lax.all_to_all(jnp.broadcast_to(charge[None], (dom_count, 1, LANES)), "dom", 0, 0, tiled=True)
    from_below = lax.ppermute(upper, "dom", up)
    from_above = lax.ppermute(lower, "dom", down)
    charge = charge.sum(axis=0)
    core = jnp.concatenate([core[:8] + from_below[:8], core[8:24], core[24:] + from_above[:8]], axis=0)
    smooth = smooth + jnp.concatenate([from_below[8:], from_above[8:]], axis=0)
    sent = jnp.concatenate(
        [core[:, None], smooth[:, None], jnp.broadcast_to(charge[None], (orb_count, 1, LANES))], axis=2
    )
    arrived = lax.all_to_all(sent, "orb", 0, 0, tiled=True)
    total = arrived.sum(axis=0)
    density = total[:, :CELLS]
    average = total[:, 2 * CELLS : 2 * CELLS + 1] / (dom_count * CORE * CELLS)
    return total[:, CELLS : 2 * CELLS] - (SWEEPS * SOURCE) * average - EXCHANGE_FACTOR * jnp.cbrt(density)


def solution(mesh):
    placed = (
        P("dom", "orb", None, None),
        P("dom", "orb"),
        P("dom"),
        P("dom", None),
        P("dom", None, None),
        P("dom", None, None),
        P(("dom", "orb"), None),
    )
    return jax.shard_map(
        body, mesh=mesh, in_specs=placed, out_specs=P(("dom", "orb"), None), check_vma=False
    )
```

```python
import functools

import jax
import jax.numpy as jnp
import ml_dtypes
import numpy as np
from jax import lax
from jax.experimental import pallas as pl
from jax.experimental.pallas import tpu as pltpu
from jax.sharding import PartitionSpec as P

SIDE = 48
CORE = 32
BUF = 8
DEGREE = 8
SWEEPS = 4
BOX = 48
CELLS = SIDE * SIDE
LANES = 128
COLS = CELLS // LANES
PAD = 8
SHIFT = 12
UP = 20
BLOCK = 384
BLOCKS = CELLS // BLOCK
DEPTH = BLOCK + LANES
TILE = 16

EXCHANGE_FACTOR = (3.0 / 3.141592653589793) ** (1.0 / 3.0)
FOUR_PI = 4.0 * 3.141592653589793
RELAXATION = 0.8
CUTOFF = 1.5
KEEP = 1.0 - RELAXATION
SPREAD = RELAXATION / 6.0
SOURCE = SPREAD * FOUR_PI


def neighbour_matrix():
    rows = np.arange(DEPTH)[:, None]
    cols = np.arange(BLOCK)[None, :]
    edge = rows - BLOCK
    after = edge < SIDE
    before = edge >= LANES - SIDE
    row_y = np.where(rows < BLOCK, rows // SIDE, np.where(after, BLOCK // SIDE, np.where(before, -1, -9)))
    row_x = np.where(rows < BLOCK, rows % SIDE, np.where(after, edge, edge - (LANES - SIDE)))
    gap_x = np.abs(row_x - cols % SIDE)
    along = (row_y == cols // SIDE) & ((gap_x == 1) | (gap_x == SIDE - 1))
    across = (gap_x == 0) & (np.abs(row_y - cols // SIDE) == 1)
    ones = (along | across).astype(ml_dtypes.bfloat16)
    return np.concatenate([ones, ones], axis=0)


def tile_of(ref, start):
    return [ref[pl.ds(start, 8), pl.ds(LANES * i, LANES)] for i in range(COLS)]


def put_tile(ref, start, pieces):
    for i in range(COLS):
        ref[pl.ds(start, 8), pl.ds(LANES * i, LANES)] = pieces[i]


def put_split(split_ref, planes, start, upper, lower):
    lane = lax.broadcasted_iota(jnp.int32, (TILE, LANES), 1)
    both = [jnp.concatenate([upper[i], lower[i]], axis=0) for i in range(COLS)]
    high = [x.astype(jnp.bfloat16) for x in both]
    low = [(both[i] - high[i].astype(jnp.float32)).astype(jnp.bfloat16) for i in range(COLS)]
    for b in range(BLOCKS):
        rows = pl.ds(b * planes + start, TILE)
        for k, half in enumerate((high, low)):
            base = k * DEPTH
            for j in range(3):
                split_ref[rows, pl.ds(base + LANES * j, LANES)] = half[3 * b + j]
            edge = jnp.where(lane < SIDE, half[(3 * b + 3) % COLS], half[(3 * b - 1) % COLS])
            split_ref[rows, pl.ds(base + BLOCK, LANES)] = edge


def multiply(split_ref, matrix_ref, sum_ref, rows):
    sum_ref[0:rows, :] = jnp.dot(
        split_ref[0:rows, :], matrix_ref[...], preferred_element_type=jnp.float32
    )


def sum_tile(sum_ref, planes, start):
    return [
        sum_ref[pl.ds((i // 3) * planes + start, 8), pl.ds(LANES * (i % 3), LANES)] for i in range(COLS)
    ]


def around(flat, before, here, after):
    row = lax.broadcasted_iota(jnp.int32, (8, LANES), 0)
    out = []
    for i in range(COLS):
        lower = pltpu.roll(jnp.where(row == 7, before[i], here[i]), 1, 0)
        upper = pltpu.roll(jnp.where(row == 0, after[i], here[i]), 7, 0)
        out.append(flat[i] + (lower + upper))
    return out


def clear_pads(refs, planes):
    zero = jnp.zeros((PAD, CELLS), jnp.float32)
    for ref in refs:
        ref[0:PAD, :] = zero
        ref[PAD + planes : 2 * PAD + planes, :] = zero


def split_all(source, split_ref, planes):
    for s in range(0, planes, TILE):
        put_split(split_ref, planes, s, tile_of(source, PAD + s), tile_of(source, PAD + s + 8))


def update(source, target, split_ref, sum_ref, planes, rule):
    for s in range(0, planes, TILE):
        tiles = [tile_of(source, PAD + s + 8 * k) for k in range(-1, 3)]
        new = []
        for k in range(2):
            total = around(sum_tile(sum_ref, planes, s + 8 * k), *tiles[k : k + 3])
            new.append(rule(s + 8 * k, tiles[k + 1], total))
            put_tile(target, PAD + s + 8 * k, new[k])
        if split_ref is not None:
            put_split(split_ref, planes, s, *new)


def scaled_potential(v_tile, w_ref):
    low = high = None
    for t in range(BOX // 8):
        for v in v_tile(8 * t):
            low = v if low is None else jnp.minimum(low, v)
            high = v if high is None else jnp.maximum(high, v)
    low = jnp.min(low, keepdims=True) + CUTOFF
    high = jnp.max(high, keepdims=True) + 6.0
    center = 0.5 * (high + low)
    inverse = 1.0 / (0.5 * (high - low))
    offset = jnp.broadcast_to((3.0 - center) * (2.0 * inverse), (8, LANES))
    double = jnp.broadcast_to(2.0 * inverse, (8, LANES))
    for t in range(BOX // 8):
        put_tile(w_ref, 8 * t, [double * v + offset for v in v_tile(8 * t)])
    return jnp.broadcast_to(inverse, (8, LANES))


def run_filter(a_refs, b_refs, splits, sums, matrix_ref, w_ref, single):
    orbs = len(a_refs)

    def first_rule(q):
        def rule(r, here, total):
            w = tile_of(w_ref, r)
            return [0.5 * (w[i] * here[i] - single * total[i]) for i in range(COLS)]

        return rule

    def next_rule(q, target):
        def rule(r, here, total):
            w = tile_of(w_ref, r)
            old = tile_of(target[q], PAD + r)
            return [(w[i] * here[i] - single * total[i]) - old[i] for i in range(COLS)]

        return rule

    def step(source, target, rules, last=False):
        for q in range(orbs):
            multiply(splits[q], matrix_ref, sums[q], BLOCKS * BOX)
        for q in range(orbs):
            update(source[q], target[q], None if last else splits[q], sums[q], BOX, rules(q))

    for q in range(orbs):
        split_all(a_refs[q], splits[q], BOX)
    step(a_refs, b_refs, first_rule)

    def pair(k, carry):
        step(b_refs, a_refs, lambda q: next_rule(q, a_refs))
        step(a_refs, b_refs, lambda q: next_rule(q, b_refs))
        return carry

    lax.fori_loop(0, (DEGREE - 2) // 2, pair, 0)
    step(b_refs, a_refs, lambda q: next_rule(q, a_refs), last=True)


def norms(a_refs):
    out = []
    for ref in a_refs:
        total = [jnp.zeros((8, LANES), jnp.float32) for _ in range(3)]
        for t in range(BOX // 8):
            for i, y in enumerate(tile_of(ref, PAD + 8 * t)):
                total[i % 3] = total[i % 3] + y * y
        mean = jnp.sum(total[0] + total[1] + total[2], keepdims=True) * (1.0 / (BOX * CELLS))
        out.append(jnp.broadcast_to(lax.rsqrt(mean + 1e-06), (8, LANES)))
    return out


def density_tile(a_refs, scale, factor_ref, core_ref, weight_ref, t, share, psi_out):
    weight = jnp.broadcast_to(weight_ref[8 * t : 8 * t + 8, :], (8, LANES))
    total = [share * c for c in tile_of(core_ref, 8 * t)]
    for q, ref in enumerate(a_refs):
        y = [p * scale[q] for p in tile_of(ref, PAD + 8 * t)]
        if psi_out is not None:
            put_tile(psi_out.at[q], 8 * t, y)
        total = [total[i] + factor_ref[q] * (y[i] * y[i]) for i in range(COLS)]
    return [weight * d for d in total]


def place_plane(g_ref, plane, row, wanted):
    @pl.when(wanted)
    def _():
        g_ref[pl.ds(PAD + row, 1), :] = plane[...]


def relax(g_ref, h_ref, d_ref, split_ref, sum_ref, matrix_ref):
    def rule(r, here, total):
        push = tile_of(d_ref, r)
        return [KEEP * here[i] + SPREAD * total[i] + SOURCE * push[i] for i in range(COLS)]

    def one(source, target, last=False):
        multiply(split_ref, matrix_ref, sum_ref, BLOCKS * BOX)
        update(source, target, None if last else split_ref, sum_ref, BOX, rule)

    split_all(g_ref, split_ref, BOX)
    for k in range(SWEEPS // 2):
        one(g_ref, h_ref)
        one(h_ref, g_ref, last=k == SWEEPS // 2 - 1)


def first_filter(
    share, factor_ref, orbitals_ref, ext_ref, core_ref, matrix_hbm, weight_ref, guess_ref,
    psi_out, density_out, up_out,
    a0, a1, b0, b1, x0, x1, s0, s1, w_ref, matrix_ref, v_ref, c_ref, sem,
):
    copies = [
        pltpu.make_async_copy(ext_ref.at[0], v_ref, sem.at[0]),
        pltpu.make_async_copy(orbitals_ref.at[0, 0], a0.at[PAD : PAD + BOX], sem.at[1]),
        pltpu.make_async_copy(orbitals_ref.at[0, 1], a1.at[PAD : PAD + BOX], sem.at[2]),
        pltpu.make_async_copy(matrix_hbm, matrix_ref, sem.at[3]),
        pltpu.make_async_copy(core_ref.at[0], c_ref, sem.at[4]),
    ]
    for copy in copies:
        copy.start()
    clear_pads((a0, a1, b0, b1), BOX)
    copies[0].wait()
    single = scaled_potential(lambda r: tile_of(v_ref, r), w_ref)
    for copy in copies[1:4]:
        copy.wait()
    run_filter((a0, a1), (b0, b1), (x0, x1), (s0, s1), matrix_ref, w_ref, single)
    scale = norms((a0, a1))
    copies[4].wait()
    for t in range(BOX // 8):
        put_tile(density_out, 8 * t, density_tile((a0, a1), scale, factor_ref, c_ref, weight_ref, t, share, psi_out))
    up_out[0:1, :] = guess_ref[...]
    up_out[1:24, :] = density_out[25:48, :]


def first_relax(rank_ref, density_ref, behind_ref, guess_ref, matrix_ref, out_ref, g_ref, h_ref, d_ref, x0, s0):
    clear_pads((g_ref, h_ref), BOX)
    rank = rank_ref[0]
    row = lax.broadcasted_iota(jnp.int32, (8, LANES), 0)
    for t in range(BOX // 8):
        total = None
        if t >= 1:
            total = tile_of(density_ref, 8 * (t - 1))
        if t < 3:
            behind = tile_of(behind_ref, 8 * t)
            if t == 0:
                total = [jnp.where(row > 0, b, 0.0) for b in behind]
            else:
                total = [total[i] + behind[i] for i in range(COLS)]
        put_tile(d_ref, 8 * t, total)
    g_ref[PAD : PAD + BOX, :] = jnp.zeros((BOX, CELLS), jnp.float32)
    g_ref[pl.ds(PAD + 16 + rank, 1), :] = guess_ref[...]
    place_plane(g_ref, behind_ref.at[0:1, :], rank - 16, rank >= 16)
    relax(g_ref, h_ref, d_ref, x0, s0, matrix_ref)
    low = 16 - SHIFT
    for p in range(CORE):
        out_ref[p, :, 0:CELLS] = d_ref[low + p : low + p + 1, :]
        out_ref[p, :, CELLS : 2 * CELLS] = g_ref[PAD + low + p : PAD + low + p + 1, :]


def second_filter(
    share, factor_ref, psi_ref, ext_ref, core_ref, weight_ref, low_ref, high_ref, owned_ref, matrix_ref,
    density_out, up_out, down_out, charge_out,
    a0, a1, b0, b1, x0, x1, s0, s1, w_ref, v_ref,
):
    clear_pads((a0, a1, b0, b1), BOX)
    a0[PAD : PAD + BOX, :] = psi_ref[0]
    a1[PAD : PAD + BOX, :] = psi_ref[1]
    first = SHIFT - BUF
    v_ref[0 : CORE - first, :] = low_ref[first:CORE, :]
    v_ref[CORE - first : BOX, :] = high_ref[0:UP, :]
    for t in range(BOX // 8):
        ionic = tile_of(ext_ref, 8 * t)
        own = tile_of(v_ref, 8 * t)
        put_tile(v_ref, 8 * t, [ionic[i] + own[i] for i in range(COLS)])
    single = scaled_potential(lambda r: tile_of(v_ref, r), w_ref)
    run_filter((a0, a1), (b0, b1), (x0, x1), (s0, s1), matrix_ref, w_ref, single)
    scale = norms((a0, a1))
    charge = [jnp.zeros((8, LANES), jnp.float32) for _ in range(3)]
    for t in range(BOX // 8):
        tile = density_tile((a0, a1), scale, factor_ref, core_ref, weight_ref, t, share, None)
        put_tile(density_out, 8 * t, tile)
        for i, d in enumerate(tile):
            charge[i % 3] = charge[i % 3] + d
    charge = jnp.sum(charge[0] + charge[1] + charge[2], keepdims=True) + jnp.sum(owned_ref[...], keepdims=True)
    charge_out[...] = jnp.broadcast_to(charge[None], charge_out.shape)
    down_out[...] = density_out[0:16, :]
    up_out[...] = density_out[32:48, :]


def second_relax(
    rank_ref, density_ref, below_ref, above_ref, plane_ref, high_ref, charge_ref, matrix_ref, out_ref,
    g_ref, h_ref, d_ref, x0, s0,
):
    clear_pads((g_ref, h_ref), BOX)
    rank = rank_ref[0]
    for t in range(BOX // 8):
        total = tile_of(density_ref, 8 * t)
        if t < 2:
            below = tile_of(below_ref, 8 * t)
            total = [total[i] + below[i] for i in range(COLS)]
        if t >= 4:
            above = tile_of(above_ref, 8 * (t - 4))
            total = [total[i] + above[i] for i in range(COLS)]
        put_tile(d_ref, 8 * t, total)
    g_ref[PAD : PAD + BOX, :] = jnp.zeros((BOX, CELLS), jnp.float32)
    place_plane(g_ref, plane_ref, rank - (SHIFT - BUF), rank >= SHIFT - BUF)
    place_plane(g_ref, high_ref.at[UP : UP + 1, :], rank + CORE - SHIFT + BUF, rank < BOX - (CORE - SHIFT + BUF))
    relax(g_ref, h_ref, d_ref, x0, s0, matrix_ref)
    for p in range(CORE):
        out_ref[p, :, 0:CELLS] = d_ref[BUF + p : BUF + p + 1, :]
        out_ref[p, :, CELLS : 2 * CELLS] = g_ref[PAD + BUF + p : PAD + BUF + p + 1, :]
        out_ref[p, :, 2 * CELLS : 2 * CELLS + LANES] = charge_ref[...]


VMEM = pl.BlockSpec(memory_space=pltpu.VMEM)
SMEM = pl.BlockSpec(memory_space=pltpu.SMEM)
HBM = pl.BlockSpec(memory_space=pltpu.HBM)
LIMIT = pltpu.CompilerParams(vmem_limit_bytes=48 * 2**20)


def f32(*shape):
    return jax.ShapeDtypeStruct(shape, jnp.float32)


def body(orbitals, occupations, occupied_count, weights, external_potential, core_density, hartree_guess):
    orb_count = lax.axis_size("orb")
    dom_count = lax.axis_size("dom")
    orb_rank = lax.axis_index("orb")
    per_device = orbitals.shape[1]
    rank = orb_rank * per_device + jnp.arange(per_device, dtype=jnp.int32)
    factors = jnp.where(rank < occupied_count[0], occupations[0], jnp.float32(0.0)) / (per_device * orb_count)
    weight = weights.reshape(BOX, 1)
    place = orb_rank.reshape(1)
    share = 1.0 / orb_count
    up = [(i, (i + 1) % dom_count) for i in range(dom_count)]
    down = [(j, i) for i, j in up]
    matrix = jnp.asarray(neighbour_matrix())
    padded = pltpu.VMEM((BOX + 2 * PAD, CELLS), jnp.float32)
    split = pltpu.VMEM((BLOCKS * BOX, 2 * DEPTH), jnp.bfloat16)
    sums = pltpu.VMEM((BLOCKS * BOX, BLOCK), jnp.float32)
    box = pltpu.VMEM((BOX, CELLS), jnp.float32)
    whole = pltpu.VMEM((2 * DEPTH, BLOCK), jnp.bfloat16)
    filter_scratch = [padded] * 4 + [split] * 2 + [sums] * 2 + [box]
    relax_scratch = [padded, padded, box, split, sums]

    psi, density, upper = pl.pallas_call(
        functools.partial(first_filter, share),
        in_specs=[SMEM] + [HBM] * 4 + [VMEM] * 2,
        out_specs=[VMEM] * 3,
        out_shape=[f32(per_device, BOX, CELLS), f32(BOX, CELLS), f32(24, CELLS)],
        scratch_shapes=filter_scratch + [whole, box, box, pltpu.SemaphoreType.DMA((5,))],
        compiler_params=LIMIT,
        name="first_filter",
    )(factors, orbitals, external_potential, core_density, matrix, weight, hartree_guess)

    behind = lax.ppermute(upper, "dom", up)
    sent = pl.pallas_call(
        first_relax,
        in_specs=[SMEM] + [VMEM] * 4,
        out_specs=VMEM,
        out_shape=f32(orb_count, 1, 2 * CELLS),
        scratch_shapes=relax_scratch,
        compiler_params=LIMIT,
        name="first_relax",
    )(place, density, behind, hartree_guess, matrix)
    total = lax.all_to_all(sent, "orb", 0, 0, tiled=True).sum(axis=0)
    owned_density = total[:, :CELLS]
    owned_hartree = total[:, CELLS:]
    plane = owned_hartree - EXCHANGE_FACTOR * jnp.cbrt(owned_density)
    low = lax.all_to_all(jnp.broadcast_to(plane[None], (orb_count, 1, CELLS)), "orb", 0, 0, tiled=True)
    low = low.reshape(CORE, CELLS)
    high = lax.ppermute(jnp.concatenate([low[:UP], owned_hartree], axis=0), "dom", down)

    density, upper, lower, charge = pl.pallas_call(
        functools.partial(second_filter, share),
        in_specs=[SMEM] + [VMEM] * 8,
        out_specs=[VMEM] * 4,
        out_shape=[f32(BOX, CELLS), f32(16, CELLS), f32(16, CELLS), f32(dom_count, 1, LANES)],
        scratch_shapes=filter_scratch + [box],
        compiler_params=LIMIT,
        name="second_filter",
    )(factors, psi, external_potential[0], core_density[0], weight, low, high, owned_density, matrix)

    charge = lax.all_to_all(charge, "dom", 0, 0, tiled=True).sum(axis=0)
    from_below = lax.ppermute(upper, "dom", up)
    from_above = lax.ppermute(lower, "dom", down)
    sent = pl.pallas_call(
        second_relax,
        in_specs=[SMEM] + [VMEM] * 7,
        out_specs=VMEM,
        out_shape=f32(orb_count, 1, 2 * CELLS + LANES),
        scratch_shapes=relax_scratch,
        compiler_params=LIMIT,
        name="second_relax",
    )(place, density, from_below, from_above, owned_hartree, high, charge, matrix)
    total = lax.all_to_all(sent, "orb", 0, 0, tiled=True).sum(axis=0)
    density = total[:, :CELLS]
    average = total[:, 2 * CELLS : 2 * CELLS + 1] / (dom_count * CORE * CELLS)
    return total[:, CELLS : 2 * CELLS] - (SWEEPS * SOURCE) * average - EXCHANGE_FACTOR * jnp.cbrt(density)


def solution(mesh):
    placed = (
        P("dom", "orb", None, None),
        P("dom", "orb"),
        P("dom"),
        P("dom", None),
        P("dom", None, None),
        P("dom", None, None),
        P(("dom", "orb"), None),
    )
    return jax.shard_map(
        body, mesh=mesh, in_specs=placed, out_specs=P(("dom", "orb"), None), check_vma=False
    )
```

```python
import functools

import jax
import jax.numpy as jnp
import ml_dtypes
import numpy as np
from jax import lax
from jax.experimental import pallas as pl
from jax.experimental.pallas import tpu as pltpu
from jax.sharding import PartitionSpec as P

SIDE = 48
CORE = 32
BUF = 8
DEGREE = 8
SWEEPS = 4
BOX = 48
CELLS = SIDE * SIDE
LANES = 128
COLS = CELLS // LANES
PAD = 8
SHIFT = 12
UP = 20
PERIOD = 768
GROUPS = CELLS // PERIOD
WIDTH = 256
DEPTH = WIDTH + 2 * LANES
TILE = 16

EXCHANGE_FACTOR = (3.0 / 3.141592653589793) ** (1.0 / 3.0)
FOUR_PI = 4.0 * 3.141592653589793
RELAXATION = 0.8
CUTOFF = 1.5
KEEP = 1.0 - RELAXATION
SPREAD = RELAXATION / 6.0
SOURCE = SPREAD * FOUR_PI


def neighbour_matrix():
    parts = []
    for r in range(PERIOD // WIDTH):
        rows = (WIDTH * r - LANES + np.arange(DEPTH))[:, None]
        cols = (WIDTH * r + np.arange(WIDTH))[None, :]
        gap_x = np.abs(rows % SIDE - cols % SIDE)
        gap_y = np.abs(rows // SIDE - cols // SIDE)
        along = (gap_y == 0) & ((gap_x == 1) | (gap_x == SIDE - 1))
        parts.append((along | ((gap_x == 0) & (gap_y == 1))).astype(ml_dtypes.bfloat16))
    return np.stack(parts)


def tile_of(ref, start):
    return [ref[pl.ds(start, 8), pl.ds(LANES * i, LANES)] for i in range(COLS)]


def put_tile(ref, start, pieces):
    for i in range(COLS):
        ref[pl.ds(start, 8), pl.ds(LANES * i, LANES)] = pieces[i]


def put_split(split_ref, start, upper, lower):
    both = [jnp.concatenate([upper[i], lower[i]], axis=0) for i in range(COLS)]
    high = [x.astype(jnp.bfloat16) for x in both]
    low = [(both[i] - high[i].astype(jnp.float32)).astype(jnp.bfloat16) for i in range(COLS)]
    span = PERIOD // LANES
    for g in range(GROUPS):
        for k, half in enumerate((high, low)):
            rows = pl.ds((2 * g + k) * BOX + start, TILE)
            for j in range(span + 2):
                split_ref[rows, pl.ds(LANES * j, LANES)] = half[(span * g + j - 1) % COLS]


def multiply(split_ref, matrix_ref, sum_ref):
    for r in range(PERIOD // WIDTH):
        sum_ref[:, WIDTH * r : WIDTH * (r + 1)] = jnp.dot(
            split_ref[:, WIDTH * r : WIDTH * r + DEPTH], matrix_ref[r], preferred_element_type=jnp.float32
        )


def sum_tile(sum_ref, start):
    span = PERIOD // LANES

    def part(k, i):
        return sum_ref[pl.ds((2 * (i // span) + k) * BOX + start, 8), pl.ds(LANES * (i % span), LANES)]

    return [part(0, i) + part(1, i) for i in range(COLS)]


def around(flat, before, here, after):
    row = lax.broadcasted_iota(jnp.int32, (8, LANES), 0)
    out = []
    for i in range(COLS):
        lower = pltpu.roll(jnp.where(row == 7, before[i], here[i]), 1, 0)
        upper = pltpu.roll(jnp.where(row == 0, after[i], here[i]), 7, 0)
        out.append(flat[i] + (lower + upper))
    return out


def clear_pads(refs, planes):
    zero = jnp.zeros((PAD, CELLS), jnp.float32)
    for ref in refs:
        ref[0:PAD, :] = zero
        ref[PAD + planes : 2 * PAD + planes, :] = zero


def split_all(source, split_ref, planes):
    for s in range(0, planes, TILE):
        put_split(split_ref, s, tile_of(source, PAD + s), tile_of(source, PAD + s + 8))


def update(source, target, split_ref, sum_ref, planes, rule):
    for s in range(0, planes, TILE):
        tiles = [tile_of(source, PAD + s + 8 * k) for k in range(-1, 3)]
        new = []
        for k in range(2):
            total = around(sum_tile(sum_ref, s + 8 * k), *tiles[k : k + 3])
            new.append(rule(s + 8 * k, tiles[k + 1], total))
            put_tile(target, PAD + s + 8 * k, new[k])
        if split_ref is not None:
            put_split(split_ref, s, *new)


def scaled_potential(v_tile, w_ref):
    low = high = None
    for t in range(BOX // 8):
        for v in v_tile(8 * t):
            low = v if low is None else jnp.minimum(low, v)
            high = v if high is None else jnp.maximum(high, v)
    low = jnp.min(low, keepdims=True) + CUTOFF
    high = jnp.max(high, keepdims=True) + 6.0
    center = 0.5 * (high + low)
    inverse = 1.0 / (0.5 * (high - low))
    offset = jnp.broadcast_to((3.0 - center) * (2.0 * inverse), (8, LANES))
    double = jnp.broadcast_to(2.0 * inverse, (8, LANES))
    for t in range(BOX // 8):
        put_tile(w_ref, 8 * t, [double * v + offset for v in v_tile(8 * t)])
    return jnp.broadcast_to(inverse, (8, LANES))


def run_filter(a_refs, b_refs, splits, sums, matrix_ref, w_ref, single):
    orbs = len(a_refs)

    def first_rule(q):
        def rule(r, here, total):
            w = tile_of(w_ref, r)
            return [0.5 * (w[i] * here[i] - single * total[i]) for i in range(COLS)]

        return rule

    def next_rule(q, target):
        def rule(r, here, total):
            w = tile_of(w_ref, r)
            old = tile_of(target[q], PAD + r)
            return [(w[i] * here[i] - single * total[i]) - old[i] for i in range(COLS)]

        return rule

    def step(source, target, rules, last=False):
        for q in range(orbs):
            multiply(splits[q], matrix_ref, sums[q])
        for q in range(orbs):
            update(source[q], target[q], None if last else splits[q], sums[q], BOX, rules(q))

    for q in range(orbs):
        split_all(a_refs[q], splits[q], BOX)
    step(a_refs, b_refs, first_rule)

    def pair(k, carry):
        step(b_refs, a_refs, lambda q: next_rule(q, a_refs))
        step(a_refs, b_refs, lambda q: next_rule(q, b_refs))
        return carry

    lax.fori_loop(0, (DEGREE - 2) // 2, pair, 0)
    step(b_refs, a_refs, lambda q: next_rule(q, a_refs), last=True)


def norms(a_refs):
    out = []
    for ref in a_refs:
        total = [jnp.zeros((8, LANES), jnp.float32) for _ in range(3)]
        for t in range(BOX // 8):
            for i, y in enumerate(tile_of(ref, PAD + 8 * t)):
                total[i % 3] = total[i % 3] + y * y
        mean = jnp.sum(total[0] + total[1] + total[2], keepdims=True) * (1.0 / (BOX * CELLS))
        out.append(jnp.broadcast_to(lax.rsqrt(mean + 1e-06), (8, LANES)))
    return out


def occupation_factors(rank_ref, count_ref, occupation_ref, orbs, total):
    rank = rank_ref[0] * orbs
    return [
        jnp.where(rank + q < count_ref[0], occupation_ref[0, q], jnp.float32(0.0)) * (1.0 / total)
        for q in range(orbs)
    ]


def density_tile(a_refs, scale, factor, core_ref, weight_ref, t, share, psi_out):
    row = lax.broadcasted_iota(jnp.int32, (8, BOX), 0)
    column = lax.broadcasted_iota(jnp.int32, (8, BOX), 1)
    weight = jnp.where(column == row + 8 * t, jnp.broadcast_to(weight_ref[...], (8, BOX)), 0.0)
    weight = jnp.broadcast_to(jnp.sum(weight, axis=1, keepdims=True), (8, LANES))
    total = [share * c for c in tile_of(core_ref, 8 * t)]
    for q, ref in enumerate(a_refs):
        y = [p * scale[q] for p in tile_of(ref, PAD + 8 * t)]
        if psi_out is not None:
            put_tile(psi_out.at[q], 8 * t, y)
        total = [total[i] + factor[q] * (y[i] * y[i]) for i in range(COLS)]
    return [weight * d for d in total]


def place_plane(g_ref, plane, row, wanted):
    @pl.when(wanted)
    def _():
        g_ref[pl.ds(PAD + row, 1), :] = plane[...]


def relax(g_ref, h_ref, d_ref, split_ref, sum_ref, matrix_ref):
    def rule(r, here, total):
        push = tile_of(d_ref, r)
        return [KEEP * here[i] + SPREAD * total[i] + SOURCE * push[i] for i in range(COLS)]

    def one(source, target, last=False):
        multiply(split_ref, matrix_ref, sum_ref)
        update(source, target, None if last else split_ref, sum_ref, BOX, rule)

    split_all(g_ref, split_ref, BOX)
    for k in range(SWEEPS // 2):
        one(g_ref, h_ref)
        one(h_ref, g_ref, last=k == SWEEPS // 2 - 1)


def first_filter(
    orb_count, rank_ref, count_ref, occupation_ref, orbitals_ref, ext_ref, core_ref, matrix_hbm, weight_ref, guess_ref,
    psi_out, density_out, up_out,
    a0, a1, b0, b1, x0, x1, s0, s1, w_ref, matrix_ref, v_ref, c_ref, sem,
):
    copies = [
        pltpu.make_async_copy(ext_ref.at[0], v_ref, sem.at[0]),
        pltpu.make_async_copy(orbitals_ref.at[0, 0], a0.at[PAD : PAD + BOX], sem.at[1]),
        pltpu.make_async_copy(orbitals_ref.at[0, 1], a1.at[PAD : PAD + BOX], sem.at[2]),
        pltpu.make_async_copy(matrix_hbm, matrix_ref, sem.at[3]),
        pltpu.make_async_copy(core_ref.at[0], c_ref, sem.at[4]),
    ]
    for copy in copies:
        copy.start()
    clear_pads((a0, a1, b0, b1), BOX)
    copies[0].wait()
    single = scaled_potential(lambda r: tile_of(v_ref, r), w_ref)
    for copy in copies[1:4]:
        copy.wait()
    run_filter((a0, a1), (b0, b1), (x0, x1), (s0, s1), matrix_ref, w_ref, single)
    scale = norms((a0, a1))
    factor = occupation_factors(rank_ref, count_ref, occupation_ref, 2, 2 * orb_count)
    copies[4].wait()
    for t in range(BOX // 8):
        put_tile(density_out, 8 * t, density_tile((a0, a1), scale, factor, c_ref, weight_ref, t, 1.0 / orb_count, psi_out))
    up_out[0:1, :] = guess_ref[...]
    up_out[1:24, :] = density_out[25:48, :]


def first_relax(rank_ref, density_ref, behind_ref, guess_ref, matrix_ref, out_ref, g_ref, h_ref, d_ref, x0, s0):
    clear_pads((g_ref, h_ref), BOX)
    rank = rank_ref[0]
    row = lax.broadcasted_iota(jnp.int32, (8, LANES), 0)
    for t in range(BOX // 8):
        total = None
        if t >= 1:
            total = tile_of(density_ref, 8 * (t - 1))
        if t < 3:
            behind = tile_of(behind_ref, 8 * t)
            if t == 0:
                total = [jnp.where(row > 0, b, 0.0) for b in behind]
            else:
                total = [total[i] + behind[i] for i in range(COLS)]
        put_tile(d_ref, 8 * t, total)
    g_ref[PAD : PAD + BOX, :] = jnp.zeros((BOX, CELLS), jnp.float32)
    g_ref[pl.ds(PAD + 16 + rank, 1), :] = guess_ref[...]
    place_plane(g_ref, behind_ref.at[0:1, :], rank - 16, rank >= 16)
    relax(g_ref, h_ref, d_ref, x0, s0, matrix_ref)
    low = 16 - SHIFT
    for p in range(CORE):
        out_ref[p, :, 0:CELLS] = d_ref[low + p : low + p + 1, :]
        out_ref[p, :, CELLS : 2 * CELLS] = g_ref[PAD + low + p : PAD + low + p + 1, :]


def second_filter(
    orb_count, rank_ref, count_ref, occupation_ref, psi_ref, ext_ref, core_ref, weight_ref, low_ref, high_ref, owned_ref, matrix_ref,
    density_out, up_out, down_out, charge_out,
    a0, a1, b0, b1, x0, x1, s0, s1, w_ref, v_ref,
):
    clear_pads((a0, a1, b0, b1), BOX)
    a0[PAD : PAD + BOX, :] = psi_ref[0]
    a1[PAD : PAD + BOX, :] = psi_ref[1]
    first = SHIFT - BUF
    v_ref[0 : CORE - first, :] = low_ref[first:CORE, :]
    v_ref[CORE - first : BOX, :] = high_ref[0:UP, :]
    for t in range(BOX // 8):
        ionic = tile_of(ext_ref, 8 * t)
        own = tile_of(v_ref, 8 * t)
        put_tile(v_ref, 8 * t, [ionic[i] + own[i] for i in range(COLS)])
    single = scaled_potential(lambda r: tile_of(v_ref, r), w_ref)
    run_filter((a0, a1), (b0, b1), (x0, x1), (s0, s1), matrix_ref, w_ref, single)
    scale = norms((a0, a1))
    factor = occupation_factors(rank_ref, count_ref, occupation_ref, 2, 2 * orb_count)
    charge = [jnp.zeros((8, LANES), jnp.float32) for _ in range(3)]
    for t in range(BOX // 8):
        tile = density_tile((a0, a1), scale, factor, core_ref, weight_ref, t, 1.0 / orb_count, None)
        put_tile(density_out, 8 * t, tile)
        for i, d in enumerate(tile):
            charge[i % 3] = charge[i % 3] + d
    charge = jnp.sum(charge[0] + charge[1] + charge[2], keepdims=True) + jnp.sum(owned_ref[...], keepdims=True)
    charge_out[...] = jnp.broadcast_to(charge[None], charge_out.shape)
    down_out[...] = density_out[0:16, :]
    up_out[...] = density_out[32:48, :]


def second_relax(
    rank_ref, density_ref, below_ref, above_ref, plane_ref, high_ref, charge_ref, matrix_ref, out_ref,
    g_ref, h_ref, d_ref, x0, s0,
):
    clear_pads((g_ref, h_ref), BOX)
    rank = rank_ref[0]
    for t in range(BOX // 8):
        total = tile_of(density_ref, 8 * t)
        if t < 2:
            below = tile_of(below_ref, 8 * t)
            total = [total[i] + below[i] for i in range(COLS)]
        if t >= 4:
            above = tile_of(above_ref, 8 * (t - 4))
            total = [total[i] + above[i] for i in range(COLS)]
        put_tile(d_ref, 8 * t, total)
    g_ref[PAD : PAD + BOX, :] = jnp.zeros((BOX, CELLS), jnp.float32)
    place_plane(g_ref, plane_ref, rank - (SHIFT - BUF), rank >= SHIFT - BUF)
    place_plane(g_ref, high_ref.at[UP : UP + 1, :], rank + CORE - SHIFT + BUF, rank < BOX - (CORE - SHIFT + BUF))
    relax(g_ref, h_ref, d_ref, x0, s0, matrix_ref)
    for p in range(CORE):
        out_ref[p, :, 0:CELLS] = d_ref[BUF + p : BUF + p + 1, :]
        out_ref[p, :, CELLS : 2 * CELLS] = g_ref[PAD + BUF + p : PAD + BUF + p + 1, :]
        out_ref[p, :, 2 * CELLS : 2 * CELLS + LANES] = charge_ref[...]


VMEM = pl.BlockSpec(memory_space=pltpu.VMEM)
SMEM = pl.BlockSpec(memory_space=pltpu.SMEM)
HBM = pl.BlockSpec(memory_space=pltpu.HBM)
LIMIT = pltpu.CompilerParams(vmem_limit_bytes=48 * 2**20)
FIRST = 62 * 2**20


def f32(*shape):
    return jax.ShapeDtypeStruct(shape, jnp.float32)


def body(orbitals, occupations, occupied_count, weights, external_potential, core_density, hartree_guess):
    orb_count = lax.axis_size("orb")
    dom_count = lax.axis_size("dom")
    orb_rank = lax.axis_index("orb")
    per_device = orbitals.shape[1]
    place = orb_rank.reshape(1)
    up = [(i, (i + 1) % dom_count) for i in range(dom_count)]
    down = [(j, i) for i, j in up]
    matrix = jnp.asarray(neighbour_matrix())
    padded = pltpu.VMEM((BOX + 2 * PAD, CELLS), jnp.float32)
    split = pltpu.VMEM((2 * GROUPS * BOX, PERIOD + 2 * LANES), jnp.bfloat16)
    sums = pltpu.VMEM((2 * GROUPS * BOX, PERIOD), jnp.float32)
    box = pltpu.VMEM((BOX, CELLS), jnp.float32)
    whole = pltpu.VMEM((PERIOD // WIDTH, DEPTH, WIDTH), jnp.bfloat16)
    filter_scratch = [padded] * 4 + [split] * 2 + [sums] * 2 + [box]
    relax_scratch = [padded, padded, box, split, sums]

    psi, density, upper = pl.pallas_call(
        functools.partial(first_filter, orb_count),
        in_specs=[SMEM] * 3 + [HBM] * 4 + [VMEM] * 2,
        out_specs=[VMEM] * 3,
        out_shape=[f32(per_device, BOX, CELLS), f32(BOX, CELLS), f32(24, CELLS)],
        scratch_shapes=filter_scratch + [whole, box, box, pltpu.SemaphoreType.DMA((5,))],
        compiler_params=pltpu.CompilerParams(vmem_limit_bytes=FIRST),
        name="first_filter",
    )(place, occupied_count, occupations, orbitals, external_potential, core_density, matrix, weights, hartree_guess)

    behind = lax.ppermute(upper, "dom", up)
    sent = pl.pallas_call(
        first_relax,
        in_specs=[SMEM] + [VMEM] * 4,
        out_specs=VMEM,
        out_shape=f32(orb_count, 1, 2 * CELLS),
        scratch_shapes=relax_scratch,
        compiler_params=LIMIT,
        name="first_relax",
    )(place, density, behind, hartree_guess, matrix)
    total = lax.all_to_all(sent, "orb", 0, 0, tiled=True).sum(axis=0)
    owned_density = total[:, :CELLS]
    owned_hartree = total[:, CELLS:]
    plane = owned_hartree - EXCHANGE_FACTOR * jnp.cbrt(owned_density)
    low = lax.all_to_all(jnp.broadcast_to(plane[None], (orb_count, 1, CELLS)), "orb", 0, 0, tiled=True)
    low = low.reshape(CORE, CELLS)
    high = lax.ppermute(jnp.concatenate([low[:UP], owned_hartree], axis=0), "dom", down)

    density, upper, lower, charge = pl.pallas_call(
        functools.partial(second_filter, orb_count),
        in_specs=[SMEM] * 3 + [VMEM] * 8,
        out_specs=[VMEM] * 4,
        out_shape=[f32(BOX, CELLS), f32(16, CELLS), f32(16, CELLS), f32(dom_count, 1, LANES)],
        scratch_shapes=filter_scratch + [box],
        compiler_params=LIMIT,
        name="second_filter",
    )(
        place, occupied_count, occupations, psi, external_potential[0], core_density[0], weights, low, high,
        owned_density, matrix,
    )

    charge = lax.all_to_all(charge, "dom", 0, 0, tiled=True).sum(axis=0)
    from_below = lax.ppermute(upper, "dom", up)
    from_above = lax.ppermute(lower, "dom", down)
    sent = pl.pallas_call(
        second_relax,
        in_specs=[SMEM] + [VMEM] * 7,
        out_specs=VMEM,
        out_shape=f32(orb_count, 1, 2 * CELLS + LANES),
        scratch_shapes=relax_scratch,
        compiler_params=LIMIT,
        name="second_relax",
    )(place, density, from_below, from_above, owned_hartree, high, charge, matrix)
    total = lax.all_to_all(sent, "orb", 0, 0, tiled=True).sum(axis=0)
    density = total[:, :CELLS]
    average = total[:, 2 * CELLS : 2 * CELLS + 1] / (dom_count * CORE * CELLS)
    return total[:, CELLS : 2 * CELLS] - (SWEEPS * SOURCE) * average - EXCHANGE_FACTOR * jnp.cbrt(density)


def solution(mesh):
    placed = (
        P("dom", "orb", None, None),
        P("dom", "orb"),
        P("dom"),
        P("dom", None),
        P("dom", None, None),
        P("dom", None, None),
        P(("dom", "orb"), None),
    )
    return jax.shard_map(
        body, mesh=mesh, in_specs=placed, out_specs=P(("dom", "orb"), None), check_vma=False
    )
```

```python
import functools

import jax
import jax.numpy as jnp
import ml_dtypes
import numpy as np
from jax import lax
from jax.experimental import pallas as pl
from jax.experimental.pallas import tpu as pltpu
from jax.sharding import PartitionSpec as P

SIDE = 48
CORE = 32
BUF = 8
DEGREE = 8
SWEEPS = 4
BOX = 48
CELLS = SIDE * SIDE
LANES = 128
COLS = CELLS // LANES
PAD = 8
SHIFT = 12
UP = 20
PERIOD = 768
GROUPS = CELLS // PERIOD
WIDTH = 256
DEPTH = WIDTH + 2 * LANES
TILE = 16

EXCHANGE_FACTOR = (3.0 / 3.141592653589793) ** (1.0 / 3.0)
FOUR_PI = 4.0 * 3.141592653589793
RELAXATION = 0.8
CUTOFF = 1.5
KEEP = 1.0 - RELAXATION
SPREAD = RELAXATION / 6.0
SOURCE = SPREAD * FOUR_PI


def neighbour_matrix():
    parts = []
    for r in range(PERIOD // WIDTH):
        rows = (WIDTH * r - LANES + np.arange(DEPTH))[:, None]
        cols = (WIDTH * r + np.arange(WIDTH))[None, :]
        gap_x = np.abs(rows % SIDE - cols % SIDE)
        gap_y = np.abs(rows // SIDE - cols // SIDE)
        along = (gap_y == 0) & ((gap_x == 1) | (gap_x == SIDE - 1))
        parts.append((along | ((gap_x == 0) & (gap_y == 1))).astype(ml_dtypes.bfloat16))
    return np.stack(parts)


def tile_of(ref, start):
    return [ref[pl.ds(start, 8), pl.ds(LANES * i, LANES)] for i in range(COLS)]


def put_tile(ref, start, pieces):
    for i in range(COLS):
        ref[pl.ds(start, 8), pl.ds(LANES * i, LANES)] = pieces[i]


def put_split(split_ref, start, upper, lower):
    both = [jnp.concatenate([upper[i], lower[i]], axis=0) for i in range(COLS)]
    high = [x.astype(jnp.bfloat16) for x in both]
    low = [(both[i] - high[i].astype(jnp.float32)).astype(jnp.bfloat16) for i in range(COLS)]
    span = PERIOD // LANES
    for g in range(GROUPS):
        for k, half in enumerate((high, low)):
            rows = pl.ds((2 * g + k) * BOX + start, TILE)
            for j in range(span + 2):
                split_ref[rows, pl.ds(LANES * j, LANES)] = half[(span * g + j - 1) % COLS]


def multiply(split_ref, matrix_ref, sum_ref, parts=range(PERIOD // WIDTH)):
    for r in parts:
        sum_ref[:, WIDTH * r : WIDTH * (r + 1)] = jnp.dot(
            split_ref[:, WIDTH * r : WIDTH * r + DEPTH], matrix_ref[r], preferred_element_type=jnp.float32
        )


def sum_tile(sum_ref, start):
    span = PERIOD // LANES

    def part(k, i):
        return sum_ref[pl.ds((2 * (i // span) + k) * BOX + start, 8), pl.ds(LANES * (i % span), LANES)]

    return [part(0, i) + part(1, i) for i in range(COLS)]


def around(flat, before, here, after):
    row = lax.broadcasted_iota(jnp.int32, (8, LANES), 0)
    out = []
    for i in range(COLS):
        lower = pltpu.roll(jnp.where(row == 7, before[i], here[i]), 1, 0)
        upper = pltpu.roll(jnp.where(row == 0, after[i], here[i]), 7, 0)
        out.append(flat[i] + (lower + upper))
    return out


def clear_pads(refs, planes):
    zero = jnp.zeros((PAD, CELLS), jnp.float32)
    for ref in refs:
        ref[0:PAD, :] = zero
        ref[PAD + planes : 2 * PAD + planes, :] = zero


def split_all(source, split_ref):
    for s in range(0, BOX, TILE):
        put_split(split_ref, s, tile_of(source, PAD + s), tile_of(source, PAD + s + 8))


def update(source, target, split_ref, sum_ref, rule, beside=None):
    for k, s in enumerate(range(0, BOX, TILE)):
        if beside is not None:
            beside(k)
        tiles = [tile_of(source, PAD + s + 8 * n) for n in range(-1, 3)]
        new = []
        for n in range(2):
            total = around(sum_tile(sum_ref, s + 8 * n), *tiles[n : n + 3])
            new.append(rule(s + 8 * n, tiles[n + 1], total))
            put_tile(target, PAD + s + 8 * n, new[n])
        if split_ref is not None:
            put_split(split_ref, s, *new)


def scaled_potential(v_tile, w_ref):
    low = high = None
    for t in range(BOX // 8):
        for v in v_tile(8 * t):
            low = v if low is None else jnp.minimum(low, v)
            high = v if high is None else jnp.maximum(high, v)
    low = jnp.min(low, keepdims=True) + CUTOFF
    high = jnp.max(high, keepdims=True) + 6.0
    center = 0.5 * (high + low)
    inverse = 1.0 / (0.5 * (high - low))
    offset = jnp.broadcast_to((3.0 - center) * (2.0 * inverse), (8, LANES))
    double = jnp.broadcast_to(2.0 * inverse, (8, LANES))
    for t in range(BOX // 8):
        put_tile(w_ref, 8 * t, [double * v + offset for v in v_tile(8 * t)])
    return jnp.broadcast_to(inverse, (8, LANES))


def run_filter(a_refs, b_refs, splits, sums, matrix_ref, w_ref, single):
    orbs = len(a_refs)

    def first_rule(q):
        def rule(r, here, total):
            w = tile_of(w_ref, r)
            return [0.5 * (w[i] * here[i] - single * total[i]) for i in range(COLS)]

        return rule

    def next_rule(q, target):
        def rule(r, here, total):
            w = tile_of(w_ref, r)
            old = tile_of(target[q], PAD + r)
            return [(w[i] * here[i] - single * total[i]) - old[i] for i in range(COLS)]

        return rule

    def step(source, target, rules, last=False):
        for q in range(orbs):
            after = (q + 1) % orbs

            def beside(k):
                multiply(splits[after], matrix_ref, sums[after], [k])

            update(
                source[q], target[q], None if last else splits[q], sums[q], rules(q),
                None if last and after == 0 else beside,
            )

    for q in range(orbs):
        split_all(a_refs[q], splits[q])
    multiply(splits[0], matrix_ref, sums[0])
    step(a_refs, b_refs, first_rule)

    def pair(k, carry):
        step(b_refs, a_refs, lambda q: next_rule(q, a_refs))
        step(a_refs, b_refs, lambda q: next_rule(q, b_refs))
        return carry

    lax.fori_loop(0, (DEGREE - 2) // 2, pair, 0)
    step(b_refs, a_refs, lambda q: next_rule(q, a_refs), last=True)


def norms(a_refs):
    out = []
    for ref in a_refs:
        total = [jnp.zeros((8, LANES), jnp.float32) for _ in range(3)]
        for t in range(BOX // 8):
            for i, y in enumerate(tile_of(ref, PAD + 8 * t)):
                total[i % 3] = total[i % 3] + y * y
        mean = jnp.sum(total[0] + total[1] + total[2], keepdims=True) * (1.0 / (BOX * CELLS))
        out.append(jnp.broadcast_to(lax.rsqrt(mean + 1e-06), (8, LANES)))
    return out


def occupation_factors(rank_ref, count_ref, occupation_ref, orbs, total):
    rank = rank_ref[0] * orbs
    return [
        jnp.where(rank + q < count_ref[0], occupation_ref[0, q], jnp.float32(0.0)) * (1.0 / total)
        for q in range(orbs)
    ]


def density_tile(a_refs, scale, factor, core_ref, weight_ref, t, share):
    row = lax.broadcasted_iota(jnp.int32, (8, BOX), 0)
    column = lax.broadcasted_iota(jnp.int32, (8, BOX), 1)
    weight = jnp.where(column == row + 8 * t, jnp.broadcast_to(weight_ref[...], (8, BOX)), 0.0)
    weight = jnp.broadcast_to(jnp.sum(weight, axis=1, keepdims=True), (8, LANES))
    total = [share * c for c in tile_of(core_ref, 8 * t)]
    for q, ref in enumerate(a_refs):
        y = [p * scale[q] for p in tile_of(ref, PAD + 8 * t)]
        total = [total[i] + factor[q] * (y[i] * y[i]) for i in range(COLS)]
    return [weight * d for d in total]


def place_plane(g_ref, plane, row, wanted):
    @pl.when(wanted)
    def _():
        g_ref[pl.ds(PAD + row, 1), :] = plane[...]


def relax(g_ref, h_ref, d_ref, split_ref, sum_ref, matrix_ref):
    def rule(r, here, total):
        push = tile_of(d_ref, r)
        return [KEEP * here[i] + SPREAD * total[i] + SOURCE * push[i] for i in range(COLS)]

    def one(source, target, last=False):
        multiply(split_ref, matrix_ref, sum_ref)
        update(source, target, None if last else split_ref, sum_ref, rule)

    split_all(g_ref, split_ref)
    for k in range(SWEEPS // 2):
        one(g_ref, h_ref)
        one(h_ref, g_ref, last=k == SWEEPS // 2 - 1)


def first_filter(
    orb_count, rank_ref, count_ref, occupation_ref, orbitals_ref, ext_ref, core_ref, matrix_hbm, weight_ref, guess_ref,
    psi_out, density_out, up_out,
    a0, a1, b0, b1, x0, x1, s0, s1, w_ref, matrix_ref, v_ref, c_ref, scale_ref, sem,
):
    third = BOX // 3
    copies = []
    for n, (source, target, first) in enumerate((
        (ext_ref.at[0], v_ref, 0), (orbitals_ref.at[0, 0], a0, PAD), (orbitals_ref.at[0, 1], a1, PAD),
        (core_ref.at[0], c_ref, 0),
    )):
        copies.append([
            pltpu.make_async_copy(
                source.at[third * k : third * (k + 1)], target.at[first + third * k : first + third * (k + 1)],
                sem.at[n, k],
            )
            for k in range(3)
        ])
    copies.append([pltpu.make_async_copy(matrix_hbm.at[k], matrix_ref.at[k], sem.at[4, k]) for k in range(3)])
    for n in (0, 1, 4, 2, 3):
        for copy in copies[n]:
            copy.start()

    def arrived(n):
        for copy in copies[n]:
            copy.wait()

    clear_pads((a0, a1, b0, b1), BOX)
    arrived(0)
    single = scaled_potential(lambda r: tile_of(v_ref, r), w_ref)
    for n in (1, 4, 2):
        arrived(n)
    run_filter((a0, a1), (b0, b1), (x0, x1), (s0, s1), matrix_ref, w_ref, single)
    leaving = [
        pltpu.make_async_copy(ref.at[PAD : PAD + BOX], psi_out.at[q, 0:BOX], sem.at[5, q])
        for q, ref in enumerate((a0, a1))
    ]
    for copy in leaving:
        copy.start()
    scale = norms((a0, a1))
    for q in range(2):
        put_tile(scale_ref, 8 * q, [scale[q]] * COLS)
        leaving.append(pltpu.make_async_copy(scale_ref.at[8 * q : 8 * q + 8], psi_out.at[q, BOX : BOX + 8], sem.at[6, q]))
        leaving[-1].start()
    factor = occupation_factors(rank_ref, count_ref, occupation_ref, 2, 2 * orb_count)
    arrived(3)
    for t in range(BOX // 8):
        put_tile(density_out, 8 * t, density_tile((a0, a1), scale, factor, c_ref, weight_ref, t, 1.0 / orb_count))
    up_out[0:1, :] = guess_ref[...]
    up_out[1:24, :] = density_out[25:48, :]
    for copy in leaving:
        copy.wait()


def first_relax(rank_ref, density_ref, behind_ref, guess_ref, matrix_ref, out_ref, g_ref, h_ref, d_ref, x0, s0):
    clear_pads((g_ref, h_ref), BOX)
    rank = rank_ref[0]
    row = lax.broadcasted_iota(jnp.int32, (8, LANES), 0)
    for t in range(BOX // 8):
        total = None
        if t >= 1:
            total = tile_of(density_ref, 8 * (t - 1))
        if t < 3:
            behind = tile_of(behind_ref, 8 * t)
            if t == 0:
                total = [jnp.where(row > 0, b, 0.0) for b in behind]
            else:
                total = [total[i] + behind[i] for i in range(COLS)]
        put_tile(d_ref, 8 * t, total)
    g_ref[PAD : PAD + BOX, :] = jnp.zeros((BOX, CELLS), jnp.float32)
    g_ref[pl.ds(PAD + 16 + rank, 1), :] = guess_ref[...]
    place_plane(g_ref, behind_ref.at[0:1, :], rank - 16, rank >= 16)
    relax(g_ref, h_ref, d_ref, x0, s0, matrix_ref)
    low = 16 - SHIFT
    for p in range(CORE):
        out_ref[p, :, 0:CELLS] = d_ref[low + p : low + p + 1, :]
        out_ref[p, :, CELLS : 2 * CELLS] = g_ref[PAD + low + p : PAD + low + p + 1, :]


def second_filter(
    orb_count, rank_ref, count_ref, occupation_ref, psi_ref, ext_ref, core_ref, weight_ref, low_ref, high_ref, owned_ref, matrix_ref,
    density_out, up_out, down_out, charge_out,
    a0, a1, b0, b1, x0, x1, s0, s1, w_ref, v_ref,
):
    clear_pads((a0, a1, b0, b1), BOX)
    for q, ref in enumerate((a0, a1)):
        scale = tile_of(psi_ref.at[q], BOX)[0]
        for t in range(BOX // 8):
            put_tile(ref, PAD + 8 * t, [y * scale for y in tile_of(psi_ref.at[q], 8 * t)])
    first = SHIFT - BUF
    v_ref[0 : CORE - first, :] = low_ref[first:CORE, :]
    v_ref[CORE - first : BOX, :] = high_ref[0:UP, :]
    for t in range(BOX // 8):
        ionic = tile_of(ext_ref, 8 * t)
        own = tile_of(v_ref, 8 * t)
        put_tile(v_ref, 8 * t, [ionic[i] + own[i] for i in range(COLS)])
    single = scaled_potential(lambda r: tile_of(v_ref, r), w_ref)
    run_filter((a0, a1), (b0, b1), (x0, x1), (s0, s1), matrix_ref, w_ref, single)
    scale = norms((a0, a1))
    factor = occupation_factors(rank_ref, count_ref, occupation_ref, 2, 2 * orb_count)
    charge = [jnp.zeros((8, LANES), jnp.float32) for _ in range(3)]
    for t in range(BOX // 8):
        tile = density_tile((a0, a1), scale, factor, core_ref, weight_ref, t, 1.0 / orb_count)
        put_tile(density_out, 8 * t, tile)
        for i, d in enumerate(tile):
            charge[i % 3] = charge[i % 3] + d
    charge = jnp.sum(charge[0] + charge[1] + charge[2], keepdims=True) + jnp.sum(owned_ref[...], keepdims=True)
    charge_out[...] = jnp.broadcast_to(charge[None], charge_out.shape)
    down_out[...] = density_out[0:16, :]
    up_out[...] = density_out[32:48, :]


def second_relax(
    rank_ref, density_ref, below_ref, above_ref, plane_ref, high_ref, charge_ref, matrix_ref, out_ref,
    g_ref, h_ref, d_ref, x0, s0,
):
    clear_pads((g_ref, h_ref), BOX)
    rank = rank_ref[0]
    for t in range(BOX // 8):
        total = tile_of(density_ref, 8 * t)
        if t < 2:
            below = tile_of(below_ref, 8 * t)
            total = [total[i] + below[i] for i in range(COLS)]
        if t >= 4:
            above = tile_of(above_ref, 8 * (t - 4))
            total = [total[i] + above[i] for i in range(COLS)]
        put_tile(d_ref, 8 * t, total)
    g_ref[PAD : PAD + BOX, :] = jnp.zeros((BOX, CELLS), jnp.float32)
    place_plane(g_ref, plane_ref, rank - (SHIFT - BUF), rank >= SHIFT - BUF)
    place_plane(g_ref, high_ref.at[UP : UP + 1, :], rank + CORE - SHIFT + BUF, rank < BOX - (CORE - SHIFT + BUF))
    relax(g_ref, h_ref, d_ref, x0, s0, matrix_ref)
    for p in range(CORE):
        out_ref[p, :, 0:CELLS] = d_ref[BUF + p : BUF + p + 1, :]
        out_ref[p, :, CELLS : 2 * CELLS] = g_ref[PAD + BUF + p : PAD + BUF + p + 1, :]
        out_ref[p, :, 2 * CELLS : 2 * CELLS + LANES] = charge_ref[...]


def keep_kernel(density_ref, weight_ref, occupation_ref, density_out, weight_out, occupation_out):
    density_out[...] = density_ref[...]
    weight_out[...] = weight_ref[...]
    occupation_out[...] = occupation_ref[...]


def last_kernel(cells_everywhere, arrived_ref, out_ref):
    total = [arrived_ref[k] for k in range(4)]
    for k in range(4, CORE):
        total[k % 4] = total[k % 4] + arrived_ref[k]
    total = (total[0] + total[1]) + (total[2] + total[3])
    density = total[:, :CELLS]
    average = total[:, 2 * CELLS : 2 * CELLS + 1] * (1.0 / cells_everywhere)
    exchange = EXCHANGE_FACTOR * jnp.exp(jnp.log(density) * (1.0 / 3.0))
    out_ref[...] = total[:, CELLS : 2 * CELLS] - (SWEEPS * SOURCE) * average - exchange


VMEM = pl.BlockSpec(memory_space=pltpu.VMEM)
SMEM = pl.BlockSpec(memory_space=pltpu.SMEM)
HBM = pl.BlockSpec(memory_space=pltpu.HBM)
LIMIT = pltpu.CompilerParams(vmem_limit_bytes=48 * 2**20)
FIRST = 62 * 2**20


def f32(*shape):
    return jax.ShapeDtypeStruct(shape, jnp.float32)


def body(orbitals, occupations, occupied_count, weights, external_potential, core_density, hartree_guess):
    orb_count = lax.axis_size("orb")
    dom_count = lax.axis_size("dom")
    orb_rank = lax.axis_index("orb")
    per_device = orbitals.shape[1]
    place = orb_rank.reshape(1)
    up = [(i, (i + 1) % dom_count) for i in range(dom_count)]
    down = [(j, i) for i, j in up]
    matrix = jnp.asarray(neighbour_matrix())
    padded = pltpu.VMEM((BOX + 2 * PAD, CELLS), jnp.float32)
    split = pltpu.VMEM((2 * GROUPS * BOX, PERIOD + 2 * LANES), jnp.bfloat16)
    sums = pltpu.VMEM((2 * GROUPS * BOX, PERIOD), jnp.float32)
    box = pltpu.VMEM((BOX, CELLS), jnp.float32)
    whole = pltpu.VMEM((PERIOD // WIDTH, DEPTH, WIDTH), jnp.bfloat16)
    filter_scratch = [padded] * 4 + [split] * 2 + [sums] * 2 + [box]
    relax_scratch = [padded, padded, box, split, sums]

    psi, density, upper = pl.pallas_call(
        functools.partial(first_filter, orb_count),
        in_specs=[SMEM] * 3 + [HBM] * 4 + [VMEM] * 2,
        out_specs=[HBM] + [VMEM] * 2,
        out_shape=[f32(per_device, BOX + 8, CELLS), f32(BOX, CELLS), f32(24, CELLS)],
        scratch_shapes=filter_scratch
        + [whole, box, box, pltpu.VMEM((16, CELLS), jnp.float32), pltpu.SemaphoreType.DMA((7, 3))],
        compiler_params=pltpu.CompilerParams(vmem_limit_bytes=FIRST),
        name="first_filter",
    )(place, occupied_count, occupations, orbitals, external_potential, core_density, matrix, weights, hartree_guess)

    behind = lax.ppermute(upper, "dom", up)
    density, near_weights, near_occupations = pl.pallas_call(
        keep_kernel,
        in_specs=[VMEM] * 3,
        out_specs=[VMEM] * 3,
        out_shape=[f32(BOX, CELLS), f32(1, BOX), f32(1, per_device)],
        compiler_params=LIMIT,
        cost_estimate=pl.CostEstimate(flops=10**6, bytes_accessed=4 * 10**6, transcendentals=0),
        name="keep",
    )(density, weights, occupations)
    sent = pl.pallas_call(
        first_relax,
        in_specs=[SMEM] + [VMEM] * 4,
        out_specs=VMEM,
        out_shape=f32(orb_count, 1, 2 * CELLS),
        scratch_shapes=relax_scratch,
        compiler_params=LIMIT,
        name="first_relax",
    )(place, density, behind, hartree_guess, matrix)
    total = lax.all_to_all(sent, "orb", 0, 0, tiled=True).sum(axis=0)
    owned_density = total[:, :CELLS]
    owned_hartree = total[:, CELLS:]
    plane = owned_hartree - EXCHANGE_FACTOR * jnp.cbrt(owned_density)
    low = lax.all_to_all(jnp.broadcast_to(plane[None], (orb_count, 1, CELLS)), "orb", 0, 0, tiled=True)
    low = low.reshape(CORE, CELLS)
    high = lax.ppermute(jnp.concatenate([low[:UP], owned_hartree], axis=0), "dom", down)

    density, upper, lower, charge = pl.pallas_call(
        functools.partial(second_filter, orb_count),
        in_specs=[SMEM] * 3 + [VMEM] * 8,
        out_specs=[VMEM] * 4,
        out_shape=[f32(BOX, CELLS), f32(16, CELLS), f32(16, CELLS), f32(dom_count, 1, LANES)],
        scratch_shapes=filter_scratch + [box],
        compiler_params=LIMIT,
        name="second_filter",
    )(
        place, occupied_count, near_occupations, psi, external_potential[0], core_density[0], near_weights, low, high,
        owned_density, matrix,
    )

    charge = lax.all_to_all(charge, "dom", 0, 0, tiled=True).sum(axis=0)
    from_below = lax.ppermute(upper, "dom", up)
    from_above = lax.ppermute(lower, "dom", down)
    sent = pl.pallas_call(
        second_relax,
        in_specs=[SMEM] + [VMEM] * 7,
        out_specs=VMEM,
        out_shape=f32(orb_count, 1, 2 * CELLS + LANES),
        scratch_shapes=relax_scratch,
        compiler_params=LIMIT,
        name="second_relax",
    )(place, density, from_below, from_above, owned_hartree, high, charge, matrix)
    arrived = lax.all_to_all(sent, "orb", 0, 0, tiled=True)
    return pl.pallas_call(
        functools.partial(last_kernel, dom_count * CORE * CELLS),
        in_specs=[VMEM],
        out_specs=VMEM,
        out_shape=f32(1, CELLS),
        compiler_params=LIMIT,
        name="last",
    )(arrived)


def solution(mesh):
    placed = (
        P("dom", "orb", None, None),
        P("dom", "orb"),
        P("dom"),
        P("dom", None),
        P("dom", None, None),
        P("dom", None, None),
        P(("dom", "orb"), None),
    )
    return jax.shard_map(
        body, mesh=mesh, in_specs=placed, out_specs=P(("dom", "orb"), None), check_vma=False
    )
```

```python
import functools

import jax
import jax.numpy as jnp
import ml_dtypes
import numpy as np
from jax import lax
from jax.experimental import pallas as pl
from jax.experimental.pallas import tpu as pltpu
from jax.sharding import PartitionSpec as P

SIDE = 48
CORE = 32
BUF = 8
DEGREE = 8
SWEEPS = 4
BOX = 48
CELLS = SIDE * SIDE
LANES = 128
COLS = CELLS // LANES
PAD = 8
SHIFT = 12
UP = 20
PERIOD = 768
GROUPS = CELLS // PERIOD
WIDTH = 256
DEPTH = WIDTH + 2 * LANES
TILE = 16

EXCHANGE_FACTOR = (3.0 / 3.141592653589793) ** (1.0 / 3.0)
FOUR_PI = 4.0 * 3.141592653589793
RELAXATION = 0.8
CUTOFF = 1.5
KEEP = 1.0 - RELAXATION
SPREAD = RELAXATION / 6.0
SOURCE = SPREAD * FOUR_PI


def neighbour_matrix():
    parts = []
    for r in range(PERIOD // WIDTH):
        rows = (WIDTH * r - LANES + np.arange(DEPTH))[:, None]
        cols = (WIDTH * r + np.arange(WIDTH))[None, :]
        gap_x = np.abs(rows % SIDE - cols % SIDE)
        gap_y = np.abs(rows // SIDE - cols // SIDE)
        along = (gap_y == 0) & ((gap_x == 1) | (gap_x == SIDE - 1))
        parts.append((along | ((gap_x == 0) & (gap_y == 1))).astype(ml_dtypes.bfloat16))
    return np.stack(parts)


def tile_of(ref, start):
    return [ref[pl.ds(start, 8), pl.ds(LANES * i, LANES)] for i in range(COLS)]


def put_tile(ref, start, pieces):
    for i in range(COLS):
        ref[pl.ds(start, 8), pl.ds(LANES * i, LANES)] = pieces[i]


def put_split(split_ref, start, upper, lower):
    both = [jnp.concatenate([upper[i], lower[i]], axis=0) for i in range(COLS)]
    high = [x.astype(jnp.bfloat16) for x in both]
    low = [(both[i] - high[i].astype(jnp.float32)).astype(jnp.bfloat16) for i in range(COLS)]
    span = PERIOD // LANES
    for g in range(GROUPS):
        for k, half in enumerate((high, low)):
            rows = pl.ds((2 * g + k) * BOX + start, TILE)
            for j in range(span + 2):
                split_ref[rows, pl.ds(LANES * j, LANES)] = half[(span * g + j - 1) % COLS]


def multiply(split_ref, matrix_ref, sum_ref, parts=range(PERIOD // WIDTH)):
    for r in parts:
        sum_ref[:, WIDTH * r : WIDTH * (r + 1)] = jnp.dot(
            split_ref[:, WIDTH * r : WIDTH * r + DEPTH], matrix_ref[r], preferred_element_type=jnp.float32
        )


def sum_tile(sum_ref, start):
    span = PERIOD // LANES

    def part(k, i):
        return sum_ref[pl.ds((2 * (i // span) + k) * BOX + start, 8), pl.ds(LANES * (i % span), LANES)]

    return [part(0, i) + part(1, i) for i in range(COLS)]


def around(flat, before, here, after):
    row = lax.broadcasted_iota(jnp.int32, (8, LANES), 0)
    out = []
    for i in range(COLS):
        lower = pltpu.roll(jnp.where(row == 7, before[i], here[i]), 1, 0)
        upper = pltpu.roll(jnp.where(row == 0, after[i], here[i]), 7, 0)
        out.append(flat[i] + (lower + upper))
    return out


def clear_pads(refs, planes):
    zero = jnp.zeros((PAD, CELLS), jnp.float32)
    for ref in refs:
        ref[0:PAD, :] = zero
        ref[PAD + planes : 2 * PAD + planes, :] = zero


def split_all(source, split_ref):
    for s in range(0, BOX, TILE):
        put_split(split_ref, s, tile_of(source, PAD + s), tile_of(source, PAD + s + 8))


def update(source, target, split_ref, sum_ref, rule, beside=None):
    for k, s in enumerate(range(0, BOX, TILE)):
        if beside is not None:
            beside(k)
        tiles = [tile_of(source, PAD + s + 8 * n) for n in range(-1, 3)]
        new = []
        for n in range(2):
            total = around(sum_tile(sum_ref, s + 8 * n), *tiles[n : n + 3])
            new.append(rule(s + 8 * n, tiles[n + 1], total))
            put_tile(target, PAD + s + 8 * n, new[n])
        if split_ref is not None:
            put_split(split_ref, s, *new)


def scaled_potential(v_tile, w_ref):
    low = high = None
    for t in range(BOX // 8):
        for v in v_tile(8 * t):
            low = v if low is None else jnp.minimum(low, v)
            high = v if high is None else jnp.maximum(high, v)
    low = jnp.min(low, keepdims=True) + CUTOFF
    high = jnp.max(high, keepdims=True) + 6.0
    center = 0.5 * (high + low)
    inverse = 1.0 / (0.5 * (high - low))
    offset = jnp.broadcast_to((3.0 - center) * (2.0 * inverse), (8, LANES))
    double = jnp.broadcast_to(2.0 * inverse, (8, LANES))
    for t in range(BOX // 8):
        put_tile(w_ref, 8 * t, [double * v + offset for v in v_tile(8 * t)])
    return jnp.broadcast_to(inverse, (8, LANES))


def run_filter(a_refs, b_refs, splits, sums, matrix_ref, w_ref, single):
    orbs = len(a_refs)

    def first_rule(q):
        def rule(r, here, total):
            w = tile_of(w_ref, r)
            return [0.5 * (w[i] * here[i] - single * total[i]) for i in range(COLS)]

        return rule

    def next_rule(q, target):
        def rule(r, here, total):
            w = tile_of(w_ref, r)
            old = tile_of(target[q], PAD + r)
            return [(w[i] * here[i] - single * total[i]) - old[i] for i in range(COLS)]

        return rule

    def step(source, target, rules, last=False):
        for q in range(orbs):
            after = (q + 1) % orbs

            def beside(k):
                multiply(splits[after], matrix_ref, sums[after], [k])

            update(
                source[q], target[q], None if last else splits[q], sums[q], rules(q),
                None if last and after == 0 else beside,
            )

    for q in range(orbs):
        split_all(a_refs[q], splits[q])
    multiply(splits[0], matrix_ref, sums[0])
    step(a_refs, b_refs, first_rule)

    def pair(k, carry):
        step(b_refs, a_refs, lambda q: next_rule(q, a_refs))
        step(a_refs, b_refs, lambda q: next_rule(q, b_refs))
        return carry

    lax.fori_loop(0, (DEGREE - 2) // 2, pair, 0)
    step(b_refs, a_refs, lambda q: next_rule(q, a_refs), last=True)


def norms(a_refs):
    out = []
    for ref in a_refs:
        total = [jnp.zeros((8, LANES), jnp.float32) for _ in range(3)]
        for t in range(BOX // 8):
            for i, y in enumerate(tile_of(ref, PAD + 8 * t)):
                total[i % 3] = total[i % 3] + y * y
        mean = jnp.sum(total[0] + total[1] + total[2], keepdims=True) * (1.0 / (BOX * CELLS))
        out.append(jnp.broadcast_to(lax.rsqrt(mean + 1e-06), (8, LANES)))
    return out


def occupation_factors(rank_ref, count_ref, occupation_ref, orbs, total):
    rank = rank_ref[0] * orbs
    return [
        jnp.where(rank + q < count_ref[0], occupation_ref[0, q], jnp.float32(0.0)) * (1.0 / total)
        for q in range(orbs)
    ]


def density_tile(a_refs, scale, factor, core_ref, weight_ref, t, share, psi_out):
    row = lax.broadcasted_iota(jnp.int32, (8, BOX), 0)
    column = lax.broadcasted_iota(jnp.int32, (8, BOX), 1)
    weight = jnp.where(column == row + 8 * t, jnp.broadcast_to(weight_ref[...], (8, BOX)), 0.0)
    weight = jnp.broadcast_to(jnp.sum(weight, axis=1, keepdims=True), (8, LANES))
    total = [share * c for c in tile_of(core_ref, 8 * t)]
    for q, ref in enumerate(a_refs):
        y = [p * scale[q] for p in tile_of(ref, PAD + 8 * t)]
        if psi_out is not None:
            put_tile(psi_out.at[q], 8 * t, y)
        total = [total[i] + factor[q] * (y[i] * y[i]) for i in range(COLS)]
    return [weight * d for d in total]


def place_plane(g_ref, plane, row, wanted):
    @pl.when(wanted)
    def _():
        g_ref[pl.ds(PAD + row, 1), :] = plane[...]


def relax(g_ref, h_ref, d_ref, split_ref, sum_ref, matrix_ref):
    def rule(r, here, total):
        push = tile_of(d_ref, r)
        return [KEEP * here[i] + SPREAD * total[i] + SOURCE * push[i] for i in range(COLS)]

    def one(source, target, last=False):
        multiply(split_ref, matrix_ref, sum_ref)
        update(source, target, None if last else split_ref, sum_ref, rule)

    split_all(g_ref, split_ref)
    for k in range(SWEEPS // 2):
        one(g_ref, h_ref)
        one(h_ref, g_ref, last=k == SWEEPS // 2 - 1)


def first_filter(
    orb_count, rank_ref, count_ref, occupation_ref, orbitals_ref, ext_ref, core_ref, matrix_hbm, weight_ref, guess_ref,
    psi_out, density_out, up_out,
    a0, a1, b0, b1, x0, x1, s0, s1, w_ref, matrix_ref, v_ref, c_ref, sem,
):
    third = BOX
    copies = []
    for n, (source, target, first) in enumerate((
        (ext_ref.at[0], v_ref, 0), (orbitals_ref.at[0, 0], a0, PAD), (orbitals_ref.at[0, 1], a1, PAD),
        (core_ref.at[0], c_ref, 0),
    )):
        copies.append([
            pltpu.make_async_copy(
                source.at[third * k : third * (k + 1)], target.at[first + third * k : first + third * (k + 1)],
                sem.at[n, k],
            )
            for k in range(1)
        ])
    copies.append([pltpu.make_async_copy(matrix_hbm, matrix_ref, sem.at[4, 0])])
    def begin(*wanted):
        for n in wanted:
            for copy in copies[n]:
                copy.start()

    begin(0, 1, 2, 4)

    def arrived(n):
        for copy in copies[n]:
            copy.wait()

    clear_pads((a0, a1, b0, b1), BOX)
    arrived(0)
    single = scaled_potential(lambda r: tile_of(v_ref, r), w_ref)
    for n in (1, 2, 4):
        arrived(n)
    begin(3)
    run_filter((a0, a1), (b0, b1), (x0, x1), (s0, s1), matrix_ref, w_ref, single)
    scale = norms((a0, a1))
    factor = occupation_factors(rank_ref, count_ref, occupation_ref, 2, 2 * orb_count)
    arrived(3)
    for t in range(BOX // 8):
        put_tile(density_out, 8 * t, density_tile((a0, a1), scale, factor, c_ref, weight_ref, t, 1.0 / orb_count, psi_out))
    up_out[0:1, :] = guess_ref[...]
    up_out[1:24, :] = density_out[25:48, :]


def first_relax(rank_ref, density_ref, behind_ref, guess_ref, matrix_ref, out_ref, g_ref, h_ref, d_ref, x0, s0):
    clear_pads((g_ref, h_ref), BOX)
    rank = rank_ref[0]
    row = lax.broadcasted_iota(jnp.int32, (8, LANES), 0)
    for t in range(BOX // 8):
        total = None
        if t >= 1:
            total = tile_of(density_ref, 8 * (t - 1))
        if t < 3:
            behind = tile_of(behind_ref, 8 * t)
            if t == 0:
                total = [jnp.where(row > 0, b, 0.0) for b in behind]
            else:
                total = [total[i] + behind[i] for i in range(COLS)]
        put_tile(d_ref, 8 * t, total)
    g_ref[PAD : PAD + BOX, :] = jnp.zeros((BOX, CELLS), jnp.float32)
    g_ref[pl.ds(PAD + 16 + rank, 1), :] = guess_ref[...]
    place_plane(g_ref, behind_ref.at[0:1, :], rank - 16, rank >= 16)
    relax(g_ref, h_ref, d_ref, x0, s0, matrix_ref)
    low = 16 - SHIFT
    for p in range(CORE):
        out_ref[p, :, 0:CELLS] = d_ref[low + p : low + p + 1, :]
        out_ref[p, :, CELLS : 2 * CELLS] = g_ref[PAD + low + p : PAD + low + p + 1, :]


def second_filter(
    orb_count, rank_ref, count_ref, occupation_ref, psi_ref, ext_ref, core_ref, weight_ref, low_ref, high_ref, owned_ref, matrix_ref,
    density_out, up_out, down_out, charge_out,
    a0, a1, b0, b1, x0, x1, s0, s1, w_ref, v_ref,
):
    clear_pads((a0, a1, b0, b1), BOX)
    a0[PAD : PAD + BOX, :] = psi_ref[0]
    a1[PAD : PAD + BOX, :] = psi_ref[1]
    first = SHIFT - BUF
    v_ref[0 : CORE - first, :] = low_ref[first:CORE, :]
    v_ref[CORE - first : BOX, :] = high_ref[0:UP, :]
    for t in range(BOX // 8):
        ionic = tile_of(ext_ref, 8 * t)
        own = tile_of(v_ref, 8 * t)
        put_tile(v_ref, 8 * t, [ionic[i] + own[i] for i in range(COLS)])
    single = scaled_potential(lambda r: tile_of(v_ref, r), w_ref)
    run_filter((a0, a1), (b0, b1), (x0, x1), (s0, s1), matrix_ref, w_ref, single)
    scale = norms((a0, a1))
    factor = occupation_factors(rank_ref, count_ref, occupation_ref, 2, 2 * orb_count)
    charge = [jnp.zeros((8, LANES), jnp.float32) for _ in range(3)]
    for t in range(BOX // 8):
        tile = density_tile((a0, a1), scale, factor, core_ref, weight_ref, t, 1.0 / orb_count, None)
        put_tile(density_out, 8 * t, tile)
        for i, d in enumerate(tile):
            charge[i % 3] = charge[i % 3] + d
    charge = jnp.sum(charge[0] + charge[1] + charge[2], keepdims=True) + jnp.sum(owned_ref[...], keepdims=True)
    charge_out[...] = jnp.broadcast_to(charge[None], charge_out.shape)
    down_out[...] = density_out[0:16, :]
    up_out[...] = density_out[32:48, :]


def second_relax(
    rank_ref, density_ref, below_ref, above_ref, plane_ref, high_ref, charge_ref, matrix_ref, out_ref,
    g_ref, h_ref, d_ref, x0, s0,
):
    clear_pads((g_ref, h_ref), BOX)
    rank = rank_ref[0]
    for t in range(BOX // 8):
        total = tile_of(density_ref, 8 * t)
        if t < 2:
            below = tile_of(below_ref, 8 * t)
            total = [total[i] + below[i] for i in range(COLS)]
        if t >= 4:
            above = tile_of(above_ref, 8 * (t - 4))
            total = [total[i] + above[i] for i in range(COLS)]
        put_tile(d_ref, 8 * t, total)
    g_ref[PAD : PAD + BOX, :] = jnp.zeros((BOX, CELLS), jnp.float32)
    place_plane(g_ref, plane_ref, rank - (SHIFT - BUF), rank >= SHIFT - BUF)
    place_plane(g_ref, high_ref.at[UP : UP + 1, :], rank + CORE - SHIFT + BUF, rank < BOX - (CORE - SHIFT + BUF))
    relax(g_ref, h_ref, d_ref, x0, s0, matrix_ref)
    for p in range(CORE):
        out_ref[p, :, 0:CELLS] = d_ref[BUF + p : BUF + p + 1, :]
        out_ref[p, :, CELLS : 2 * CELLS] = g_ref[PAD + BUF + p : PAD + BUF + p + 1, :]
        out_ref[p, :, 2 * CELLS : 2 * CELLS + LANES] = charge_ref[...]


def keep_kernel(density_ref, weight_ref, occupation_ref, density_out, weight_out, occupation_out):
    density_out[...] = density_ref[...]
    weight_out[...] = weight_ref[...]
    occupation_out[...] = occupation_ref[...]


def last_kernel(cells_everywhere, arrived_ref, out_ref):
    total = [arrived_ref[k] for k in range(4)]
    for k in range(4, CORE):
        total[k % 4] = total[k % 4] + arrived_ref[k]
    total = (total[0] + total[1]) + (total[2] + total[3])
    density = total[:, :CELLS]
    average = total[:, 2 * CELLS : 2 * CELLS + 1] * (1.0 / cells_everywhere)
    exchange = EXCHANGE_FACTOR * jnp.exp(jnp.log(density) * (1.0 / 3.0))
    out_ref[...] = total[:, CELLS : 2 * CELLS] - (SWEEPS * SOURCE) * average - exchange


VMEM = pl.BlockSpec(memory_space=pltpu.VMEM)
SMEM = pl.BlockSpec(memory_space=pltpu.SMEM)
HBM = pl.BlockSpec(memory_space=pltpu.HBM)
LIMIT = pltpu.CompilerParams(vmem_limit_bytes=48 * 2**20)
FIRST = 62 * 2**20


def f32(*shape):
    return jax.ShapeDtypeStruct(shape, jnp.float32)


def body(orbitals, occupations, occupied_count, weights, external_potential, core_density, hartree_guess):
    orb_count = lax.axis_size("orb")
    dom_count = lax.axis_size("dom")
    orb_rank = lax.axis_index("orb")
    per_device = orbitals.shape[1]
    place = orb_rank.reshape(1)
    up = [(i, (i + 1) % dom_count) for i in range(dom_count)]
    down = [(j, i) for i, j in up]
    matrix = jnp.asarray(neighbour_matrix())
    padded = pltpu.VMEM((BOX + 2 * PAD, CELLS), jnp.float32)
    split = pltpu.VMEM((2 * GROUPS * BOX, PERIOD + 2 * LANES), jnp.bfloat16)
    sums = pltpu.VMEM((2 * GROUPS * BOX, PERIOD), jnp.float32)
    box = pltpu.VMEM((BOX, CELLS), jnp.float32)
    whole = pltpu.VMEM((PERIOD // WIDTH, DEPTH, WIDTH), jnp.bfloat16)
    filter_scratch = [padded] * 4 + [split] * 2 + [sums] * 2 + [box]
    relax_scratch = [padded, padded, box, split, sums]

    psi, density, upper = pl.pallas_call(
        functools.partial(first_filter, orb_count),
        in_specs=[SMEM] * 3 + [HBM] * 4 + [VMEM] * 2,
        out_specs=[VMEM] * 3,
        out_shape=[f32(per_device, BOX, CELLS), f32(BOX, CELLS), f32(24, CELLS)],
        scratch_shapes=filter_scratch + [whole, box, box, pltpu.SemaphoreType.DMA((5, 3))],
        compiler_params=pltpu.CompilerParams(vmem_limit_bytes=FIRST),
        name="first_filter",
    )(place, occupied_count, occupations, orbitals, external_potential, core_density, matrix, weights, hartree_guess)

    behind = lax.ppermute(upper, "dom", up)
    density, near_weights, near_occupations = pl.pallas_call(
        keep_kernel,
        in_specs=[VMEM] * 3,
        out_specs=[VMEM] * 3,
        out_shape=[f32(BOX, CELLS), f32(1, BOX), f32(1, per_device)],
        compiler_params=LIMIT,
        cost_estimate=pl.CostEstimate(flops=10**6, bytes_accessed=4 * 10**6, transcendentals=0),
        name="keep",
    )(density, weights, occupations)
    sent = pl.pallas_call(
        first_relax,
        in_specs=[SMEM] + [VMEM] * 4,
        out_specs=VMEM,
        out_shape=f32(orb_count, 1, 2 * CELLS),
        scratch_shapes=relax_scratch,
        compiler_params=LIMIT,
        name="first_relax",
    )(place, density, behind, hartree_guess, matrix)
    total = lax.all_to_all(sent, "orb", 0, 0, tiled=True).sum(axis=0)
    owned_density = total[:, :CELLS]
    owned_hartree = total[:, CELLS:]
    plane = owned_hartree - EXCHANGE_FACTOR * jnp.cbrt(owned_density)
    low = lax.all_to_all(jnp.broadcast_to(plane[None], (orb_count, 1, CELLS)), "orb", 0, 0, tiled=True)
    low = low.reshape(CORE, CELLS)
    high = lax.ppermute(jnp.concatenate([low[:UP], owned_hartree], axis=0), "dom", down)

    density, upper, lower, charge = pl.pallas_call(
        functools.partial(second_filter, orb_count),
        in_specs=[SMEM] * 3 + [VMEM] * 8,
        out_specs=[VMEM] * 4,
        out_shape=[f32(BOX, CELLS), f32(16, CELLS), f32(16, CELLS), f32(dom_count, 1, LANES)],
        scratch_shapes=filter_scratch + [box],
        compiler_params=LIMIT,
        name="second_filter",
    )(
        place, occupied_count, near_occupations, psi, external_potential[0], core_density[0], near_weights, low, high,
        owned_density, matrix,
    )

    charge = lax.all_to_all(charge, "dom", 0, 0, tiled=True).sum(axis=0)
    from_below = lax.ppermute(upper, "dom", up)
    from_above = lax.ppermute(lower, "dom", down)
    sent = pl.pallas_call(
        second_relax,
        in_specs=[SMEM] + [VMEM] * 7,
        out_specs=VMEM,
        out_shape=f32(orb_count, 1, 2 * CELLS + LANES),
        scratch_shapes=relax_scratch,
        compiler_params=LIMIT,
        name="second_relax",
    )(place, density, from_below, from_above, owned_hartree, high, charge, matrix)
    arrived = lax.all_to_all(sent, "orb", 0, 0, tiled=True)
    return pl.pallas_call(
        functools.partial(last_kernel, dom_count * CORE * CELLS),
        in_specs=[VMEM],
        out_specs=VMEM,
        out_shape=f32(1, CELLS),
        compiler_params=LIMIT,
        name="last",
    )(arrived)


def solution(mesh):
    placed = (
        P("dom", "orb", None, None),
        P("dom", "orb"),
        P("dom"),
        P("dom", None),
        P("dom", None, None),
        P("dom", None, None),
        P(("dom", "orb"), None),
    )
    return jax.shard_map(
        body, mesh=mesh, in_specs=placed, out_specs=P(("dom", "orb"), None), check_vma=False
    )
```
